128 devices in a mesh: fsdp: 32 (over z, y, core), rep: 4 (over x).
Axes of the slice: x: 4, y: 4, z: 4, core: 2. Of those that a mesh axis runs over, the one named last changes fastest.
Arguments:
- tokens: bfloat16 [16384, 2048], P(('fsdp', 'rep')), may hold values from -6 to 6
- cotangent: bfloat16 [16384, 2048], P(('fsdp', 'rep')), may hold values from -6 to 6
- lengths: int32 [128], P(('fsdp', 'rep')), may hold values from 26 to 128, as said below
- qkv_weight: float32 [2048, 2560], P('fsdp'), may hold values from -0.125 to 0.125
- qkv_moment: float32 [2048, 2560], P('fsdp'), may hold values from -32 to 32
- qkv_second: float32 [2048, 2560], P('fsdp'), may hold values from 2.7306666 to 10.922667
- out_weight: float32 [2048, 2048], P('fsdp'), may hold values from -0.25 to 0.25
- out_moment: float32 [2048, 2048], P('fsdp'), may hold values from -20 to 20
- out_second: float32 [2048, 2048], P('fsdp'), may hold values from 0.98304 to 3.93216
- gateup_weight: float32 [2048, 11264], P('fsdp'), may hold values from -0.125 to 0.125
- gateup_moment: float32 [2048, 11264], P('fsdp'), may hold values from -20 to 20
- gateup_second: float32 [2048, 11264], P('fsdp'), may hold values from 0.98304 to 3.93216
- down_weight: float32 [5632, 2048], P('fsdp'), may hold values from -0.078125 to 0.078125
- down_moment: float32 [5632, 2048], P('fsdp'), may hold values from -32 to 32
- down_second: float32 [5632, 2048], P('fsdp'), may hold values from 2.7306666 to 10.922667
- gains: float32 [2, 2048], replicated, may hold values from 0.5 to 1.5
- gain_moment: float32 [2, 2048], replicated, may hold values from -40 to 40
- gain_second: float32 [2, 2048], replicated, may hold values from 3.93216 to 15.72864
Outputs:
- block_output: bfloat16 [16384, 2048], P(('fsdp', 'rep'))
- input_grad: float32 [16384, 2048], P(('fsdp', 'rep'))
- qkv_moment_new: float32 [2048, 2560], P('fsdp')
- qkv_second_new: float32 [2048, 2560], P('fsdp')
- qkv_weight_new: float32 [2048, 2560], P('fsdp')
- out_moment_new: float32 [2048, 2048], P('fsdp')
- out_second_new: float32 [2048, 2048], P('fsdp')
- out_weight_new: float32 [2048, 2048], P('fsdp')
- gateup_moment_new: float32 [2048, 11264], P('fsdp')
- gateup_second_new: float32 [2048, 11264], P('fsdp')
- gateup_weight_new: float32 [2048, 11264], P('fsdp')
- down_moment_new: float32 [5632, 2048], P('fsdp')
- down_second_new: float32 [5632, 2048], P('fsdp')
- down_weight_new: float32 [5632, 2048], P('fsdp')
- gain_moment_new: float32 [2, 2048], replicated
- gain_second_new: float32 [2, 2048], replicated
- gains_new: float32 [2, 2048], replicated
The draws below stay inside these ranges and needn't reach their ends.
Inputs may be any that keep to these rules, and one draw needn't show every extreme that they name: `lengths`: each device's slots hold one sequence from slot 0; the rest are padding. the last sequence fills all 128 slots.
All inputs are finite; a program needn't handle non-finite values.
Results may differ from the reference program's by a relative error of at most 0.025.
Values may be sent and summed in bfloat16 or wider, within the bound.
No kernel may reach another device: no remote copies, remote signals or barrier semaphores. Data moves between devices by JAX's collectives and lax.ppermute only.
A program may use at most 448 MiB of HBM per device.

```python
import math
import jax
import jax.numpy as jnp
from jax import lax

D = 2048
QUERY_HEADS = 32
KEY_VALUE_HEADS = 4
HEAD_SIZE = 64
FF = 5632
TOK_DEV = 128
STEP = 10
QKV = 2560
SEQS = 128
TOKENS = 16384


def draw_lengths(key, part):
    key = jax.random.fold_in(key, 7)
    device_rank = jnp.arange(SEQS, dtype=jnp.int32)
    baseline = TOK_DEV // 3 + 2 * TOK_DEV // 3 * device_rank // max(SEQS - 1, 1)
    jitter = jax.random.randint(key, (SEQS,), 0, TOK_DEV // 8 + 1, dtype=jnp.int32)
    lengths = jnp.clip(baseline - jitter, 1, TOK_DEV)
    return lengths.at[SEQS - 1].set(TOK_DEV)


def block_scale(stream_key, shape, shards, least, largest):
    level, own = 1.0, jax.random.fold_in(stream_key, 6)
    for dim, blocks in shards:
        steps = jnp.exp(jax.random.uniform(jax.random.fold_in(own, dim), (blocks,), jnp.float32, least / len(shards), largest / len(shards)))
        level = level * jnp.repeat(steps, shape[dim] // blocks).reshape([-1 if axis == dim else 1 for axis in range(len(shape))])
    return level


def noise(own_key, dims, spread, reach, shards=(), kind=jnp.bfloat16):
    factor_of = block_scale(own_key, dims, shards, -0.22, 0.18) if shards else 1.0
    drawn = jax.random.normal(own_key, dims, jnp.float32) * spread * factor_of
    return jnp.minimum(jnp.maximum(drawn, -reach), reach).astype(kind)


def setup_inputs(seed: int = 0) -> dict:
    key_of = jax.random.split(jax.random.key(seed), 19)
    tokens = noise(key_of[0], (TOKENS, D), 1.0, 6.0, ((0, 128),))
    cotangent = noise(key_of[1], (TOKENS, D), 1.0, 6.0, ((0, 128),))
    lengths = draw_lengths(jax.random.fold_in(key_of[18], 71), 0)
    qkv_weight = noise(key_of[3], (D, QKV), D ** -0.5, 0.125, ((0, 32),), jnp.float32)
    qkv_moment = noise(key_of[4], (D, QKV), (0.111 * 0.5 * (2 * TOKENS / 3) ** 0.5), 32.0, ((0, 32),), jnp.float32)
    qkv_second = jnp.clip(jnp.exp(math.log(10.922667) - 1.3862944 * jax.random.uniform(key_of[5], (D, QKV), jnp.float32) ** block_scale(key_of[5], (D, QKV), ((0, 32),), -0.2, 0.2)), 2.7306666, 10.922667)
    out_weight = noise(key_of[6], (QUERY_HEADS * HEAD_SIZE, D), (QUERY_HEADS * HEAD_SIZE // 4) ** -0.5, 0.25, ((0, 32),), jnp.float32)
    out_moment = noise(key_of[7], (QUERY_HEADS * HEAD_SIZE, D), (0.111 * 0.3 * (2 * TOKENS / 3) ** 0.5), 20.0, ((0, 32),), jnp.float32)
    out_second = jnp.clip(jnp.exp(math.log(3.93216) - 1.3862944 * jax.random.uniform(key_of[8], (QUERY_HEADS * HEAD_SIZE, D), jnp.float32) ** block_scale(key_of[8], (QUERY_HEADS * HEAD_SIZE, D), ((0, 32),), -0.2, 0.2)), 0.98304, 3.93216)
    gateup_weight = noise(key_of[9], (D, 2 * FF), D ** -0.5, 0.125, ((0, 32),), jnp.float32)
    gateup_moment = noise(key_of[10], (D, 2 * FF), (0.111 * 0.3 * (2 * TOKENS / 3) ** 0.5), 20.0, ((0, 32),), jnp.float32)
    gateup_second = jnp.clip(jnp.exp(math.log(3.93216) - 1.3862944 * jax.random.uniform(key_of[11], (D, 2 * FF), jnp.float32) ** block_scale(key_of[11], (D, 2 * FF), ((0, 32),), -0.2, 0.2)), 0.98304, 3.93216)
    down_weight = noise(key_of[12], (FF, D), FF ** -0.5, 0.078125, ((0, 32),), jnp.float32)
    down_moment = noise(key_of[13], (FF, D), (0.111 * 0.5 * (2 * TOKENS / 3) ** 0.5), 32.0, ((0, 32),), jnp.float32)
    down_second = jnp.clip(jnp.exp(math.log(10.922667) - 1.3862944 * jax.random.uniform(key_of[14], (FF, D), jnp.float32) ** block_scale(key_of[14], (FF, D), ((0, 32),), -0.2, 0.2)), 2.7306666, 10.922667)
    gains = jnp.clip(1.0 + 0.1 * jax.random.normal(key_of[15], (2, D), jnp.float32), 0.5, 1.5)
    gain_moment = noise(key_of[16], (2, D), (0.111 * 0.6 * (2 * TOKENS / 3) ** 0.5), 40.0, (), jnp.float32)
    gain_second = jnp.clip(jnp.exp(jax.random.uniform(key_of[17], (2, D), jnp.float32, math.log(3.93216), math.log(15.72864))), 3.93216, 15.72864)
    return {"tokens": tokens, "cotangent": cotangent, "lengths": lengths, "qkv_weight": qkv_weight, "qkv_moment": qkv_moment, "qkv_second": qkv_second, "out_weight": out_weight, "out_moment": out_moment, "out_second": out_second, "gateup_weight": gateup_weight, "gateup_moment": gateup_moment, "gateup_second": gateup_second, "down_weight": down_weight, "down_moment": down_moment, "down_second": down_second, "gains": gains, "gain_moment": gain_moment, "gain_second": gain_second}


@jax.custom_vjp
def lower_cast(v):
    return lax.optimization_barrier(v.astype(jnp.bfloat16)).astype(jnp.float32)

@jax.custom_vjp
def low_back(v):
    return v

def low_keep(v):
    return (lower_cast(v), None)

def low_pass(kept, grad):
    return (grad,)

def back_keep(v):
    return (v, None)

def back_low(kept, grad):
    return (lower_cast(grad),)
lower_cast.defvjp(low_keep, low_pass)
low_back.defvjp(back_keep, back_low)
norm_epsilon = 1e-05
beta_one = 0.9
beta_two = 0.999
adam_epsilon = 1e-08
matrix_rate = 0.02
matrix_decay = 0.1
gain_rate = 0.5
masked_score = -1e+30
exact_mode = lax.Precision.HIGHEST

def rms_norm(values, gain):
    inverse = lax.rsqrt(lax.optimization_barrier(jnp.mean(values * values, axis=-1, keepdims=True)) + norm_epsilon)
    return values * inverse * gain

def rotary_tables(token_count):
    positions = jnp.arange(token_count, dtype=jnp.float32)
    exponents = jnp.arange(0, HEAD_SIZE, 2, dtype=jnp.float32) / HEAD_SIZE
    freqs = jnp.power(10000.0, -exponents)
    angles = positions[:, None] * freqs[None, :]
    angles = jnp.concatenate([angles, angles], axis=-1)[:, None, :]
    return (jnp.cos(angles), jnp.sin(angles))

def rotate_pairs(values, cosine_table, sine_table):
    half = values.shape[-1] // 2
    turned = jnp.concatenate([-values[..., half:], values[..., :half]], axis=-1)
    return values * cosine_table + turned * sine_table

def attend(parts):
    query_rows, key, value_rows = parts
    token_count = query_rows.shape[0]
    head_group = QUERY_HEADS // KEY_VALUE_HEADS
    grouped_heads = query_rows.reshape(token_count, KEY_VALUE_HEADS, head_group, HEAD_SIZE)
    scores = jnp.einsum('tkgd,skd->kgts', grouped_heads, key, precision=exact_mode) * HEAD_SIZE ** (-0.5)
    scores = low_back(scores)
    row_index = lax.broadcasted_iota(jnp.int32, (token_count, token_count), 0)
    col_index = lax.broadcasted_iota(jnp.int32, (token_count, token_count), 1)
    scores = jnp.where(row_index >= col_index, scores, masked_score)
    probs = lower_cast(jax.nn.softmax(scores, axis=-1))
    mixed = jnp.einsum('kgts,skd->tkgd', probs, value_rows, precision=exact_mode)
    return mixed.reshape(token_count, QUERY_HEADS * HEAD_SIZE)

def layer(tokens, mask, qkv_weight, out_weight, gateup_weight, down_weight, gains):
    local_sequences = mask.shape[0]
    token_count = mask.shape[1]
    model_width = QUERY_HEADS * HEAD_SIZE
    key_value_width = KEY_VALUE_HEADS * HEAD_SIZE
    normed = lower_cast(rms_norm(tokens, gains[0]))
    joined_rows = low_back(jnp.dot(normed, lower_cast(qkv_weight), precision=exact_mode))
    joined_rows = joined_rows.reshape(local_sequences, token_count, QKV)
    cosine_table, sine_table = rotary_tables(token_count)
    query_rows = lower_cast(rotate_pairs(joined_rows[..., :model_width].reshape(local_sequences, token_count, QUERY_HEADS, HEAD_SIZE), cosine_table, sine_table))
    key = lower_cast(rotate_pairs(joined_rows[..., model_width:model_width + key_value_width].reshape(local_sequences, token_count, KEY_VALUE_HEADS, HEAD_SIZE), cosine_table, sine_table))
    value_rows = lower_cast(joined_rows[..., model_width + key_value_width:].reshape(local_sequences, token_count, KEY_VALUE_HEADS, HEAD_SIZE))
    mixed = lax.map(jax.checkpoint(attend), (query_rows, key, value_rows))
    mixed = lower_cast(low_back(mixed.reshape(local_sequences * token_count, model_width)))
    branch = low_back(jnp.dot(mixed, lower_cast(out_weight), precision=exact_mode))
    middle = tokens + branch
    second = lower_cast(rms_norm(middle, gains[1]))
    both = low_back(jnp.dot(second, lower_cast(gateup_weight), precision=exact_mode))
    hidden = lower_cast(jax.nn.silu(both[:, :FF]) * both[:, FF:])
    output = low_back(jnp.dot(hidden, lower_cast(down_weight), precision=exact_mode))
    return (middle + output) * mask.reshape(-1, 1)

def adamw(weight, grad, moment, second, rate, decay):
    moment = beta_one * moment + (1.0 - beta_one) * grad
    second = beta_two * second + (1.0 - beta_two) * grad * grad
    fix_one = 1.0 - beta_one ** STEP
    fix_two = 1.0 - beta_two ** STEP
    weight = weight - rate * (moment / fix_one / (jnp.sqrt(second / fix_two) + adam_epsilon) + decay * weight)
    return (moment, second, weight)

def reference(tokens, cotangent, lengths, qkv_weight, qkv_moment, qkv_second, out_weight, out_moment, out_second, gateup_weight, gateup_moment, gateup_second, down_weight, down_moment, down_second, gains, gain_moment, gain_second):
    per_round = max(1, min(SEQS, 4096 // TOK_DEV))
    rounds = SEQS // per_round
    positions = jnp.arange(TOK_DEV, dtype=jnp.int32)
    mask = (positions[None, :] < lengths[:, None]).astype(jnp.float32)
    flat = tokens.astype(jnp.float32).reshape(rounds, per_round * TOK_DEV, D)
    backs = cotangent.astype(jnp.float32).reshape(rounds, per_round * TOK_DEV, D)
    masks = mask.reshape(rounds, per_round, TOK_DEV)
    weights = (qkv_weight, out_weight, gateup_weight, down_weight, gains)

    def one_round(totals, item):
        flat_part, back_part, mask_part = item

        def forward(token_part, *params):
            return layer(token_part, mask_part, *params)
        result, pullback = jax.vjp(forward, flat_part, *weights)
        grads = pullback(back_part)
        totals = tuple((summed + added for summed, added in zip(totals, grads[1:])))
        return (totals, (result.astype(jnp.bfloat16), grads[0]))
    initial = tuple((jnp.zeros_like(weight) for weight in weights))
    totals, (results, token_grads) = lax.scan(one_round, initial, (flat, backs, masks))
    block_output = results.reshape(TOKENS, D)
    input_grad = token_grads.reshape(TOKENS, D)
    qkv_new = adamw(qkv_weight, totals[0], qkv_moment, qkv_second, matrix_rate, matrix_decay)
    out_new = adamw(out_weight, totals[1], out_moment, out_second, matrix_rate, matrix_decay)
    gateup_new = adamw(gateup_weight, totals[2], gateup_moment, gateup_second, matrix_rate, matrix_decay)
    down_new = adamw(down_weight, totals[3], down_moment, down_second, matrix_rate, matrix_decay)
    gain_new = adamw(gains, totals[4], gain_moment, gain_second, gain_rate, 0.0)
    return (block_output, input_grad, qkv_new[0], qkv_new[1], qkv_new[2], out_new[0], out_new[1], out_new[2], gateup_new[0], gateup_new[1], gateup_new[2], down_new[0], down_new[1], down_new[2], gain_new[0], gain_new[1], gain_new[2])
```

```python
import functools

import jax
import jax.numpy as jnp
from jax import lax
from jax.experimental import pallas as pl
from jax.experimental.pallas import tpu as pltpu
from jax.sharding import Mesh
from jax.sharding import PartitionSpec as P

QUERY_HEADS = 32
KEY_VALUE_HEADS = 4
HEAD_SIZE = 64
FF = 5632
STEP = 10
GROUP = 4
WIDTH = QUERY_HEADS * HEAD_SIZE
KV_WIDTH = KEY_VALUE_HEADS * HEAD_SIZE
HEADS = QUERY_HEADS // GROUP
Q_COLS = WIDTH // GROUP
KV_COLS = KV_WIDTH // GROUP
FF_COLS = FF // GROUP
FSDP = ("fsdp_0", "fsdp_1", "fsdp_2")
FSDP_REP = ("fsdp_0", "fsdp_1", "fsdp_2", "rep")

norm_epsilon = 1e-05
beta_one = 0.9
beta_two = 0.999
adam_epsilon = 1e-08
matrix_rate = 0.02
matrix_decay = 0.1
gain_rate = 0.5
masked_score = -1e30
f32 = jnp.float32
bf16 = jnp.bfloat16

TURN = [(z * GROUP + x, x * GROUP + z) for z in range(GROUP) for x in range(GROUP)]


def dot(a, b, ca, cb):
    return lax.dot_general(a, b, (((ca,), (cb,)), ((), ())), preferred_element_type=f32)


def fetch(block, k):
    return lax.ppermute(block, "rep", [((i + k) % GROUP, i) for i in range(GROUP)])


def send(block, k):
    return lax.ppermute(block, "rep", [(i, (i + k) % GROUP) for i in range(GROUP)])


def gather_rows(block):
    return jnp.concatenate([block] + [fetch(block, k) for k in range(1, GROUP)], axis=0)


def scatter_rows(partial, rows):
    total = partial[:rows]
    low = partial.astype(bf16)
    for k in (2, 1, 3):
        total = total + send(low[k * rows : (k + 1) * rows], k).astype(f32)
    return total


def turn(piece):
    return lax.ppermute(piece, ("fsdp_0", "rep"), TURN)


def spread(block):
    return lax.all_gather(block, FSDP, axis=0, tiled=True)


def sum_along(block, axis, dim, dtype):
    here = lax.axis_index(axis)

    def entry(k):
        return lax.dynamic_index_in_dim(block, (here + k) % GROUP, dim, keepdims=False)

    total = entry(0).astype(f32)
    for k in (2, 1, 3):
        perm = [(i, (i + k) % GROUP) for i in range(GROUP)]
        total = total + lax.ppermute(entry(k), axis, perm).astype(f32)
    return total.astype(dtype)


def collect(partial, first):
    low = partial.astype(bf16).reshape(GROUP, GROUP, 2, -1, partial.shape[-1])
    core = lax.axis_index("fsdp_2")
    other = lax.dynamic_index_in_dim(low, 1 - core, 2, keepdims=False)
    own = lax.dynamic_index_in_dim(low, core, 2, keepdims=False)
    other = lax.ppermute(other, "fsdp_2", [(0, 1), (1, 0)])
    pair = (own.astype(f32) + other.astype(f32)).astype(bf16)
    if first == "fsdp_0":
        return sum_along(sum_along(pair, "fsdp_0", 0, bf16), "fsdp_1", 0, bf16)
    return sum_along(sum_along(pair, "fsdp_1", 1, bf16), "fsdp_0", 0, bf16)


def collect_far(partial):
    return lax.psum_scatter(partial.astype(bf16), FSDP, scatter_dimension=0, tiled=True)


def share(piece):
    return [piece] + [fetch(piece, k) for k in range(1, GROUP)]


def share_turned(piece):
    out = []
    for k in range(GROUP):
        perm = [
            (z * GROUP + x, x * GROUP + (z - k) % GROUP) for z in range(GROUP) for x in range(GROUP)
        ]
        out.append(lax.ppermute(piece, ("fsdp_0", "rep"), perm))
    return out


def norm_inverse(values):
    return lax.rsqrt(jnp.mean(values * values, axis=-1, keepdims=True) + norm_epsilon)


def norm_backward(values, inverse, gain, grads):
    scaled = grads * gain
    return inverse * scaled - values * (inverse * inverse * inverse) * jnp.mean(
        scaled * values, axis=-1, keepdims=True
    )


def rotary_tables(token_count):
    positions = jnp.arange(token_count, dtype=f32)
    exponents = jnp.arange(0, HEAD_SIZE, 2, dtype=f32) / HEAD_SIZE
    freqs = jnp.power(10000.0, -exponents)
    angles = positions[:, None] * freqs[None, :]
    angles = jnp.concatenate([angles, angles], axis=-1)[:, None, :]
    return (jnp.cos(angles), jnp.sin(angles))


def rotate_pairs(values, cosine_table, sine_table):
    half = values.shape[-1] // 2
    turned = jnp.concatenate([-values[..., half:], values[..., :half]], axis=-1)
    return values * cosine_table + turned * sine_table


def unrotate(values, cosine_table, sine_table):
    half = values.shape[-1] // 2
    product = values * sine_table
    turned = jnp.concatenate([product[..., half:], -product[..., :half]], axis=-1)
    return values * cosine_table + turned


def causal_scores(query, key):
    count = query.shape[1]
    scores = jnp.einsum("bthd,bsd->bhts", query, key, preferred_element_type=f32)
    scores = scores * HEAD_SIZE ** (-0.5)
    row_index = lax.broadcasted_iota(jnp.int32, (count, count), 0)
    col_index = lax.broadcasted_iota(jnp.int32, (count, count), 1)
    return jnp.where(row_index >= col_index, scores, masked_score)


def attend(query, key, value):
    scores = causal_scores(query, key)
    top = jnp.max(scores, axis=-1, keepdims=True)
    expos = jnp.exp(scores - top)
    totals = jnp.sum(expos, axis=-1, keepdims=True)
    probs = (expos / totals).astype(bf16)
    mixed = jnp.einsum("bhts,bsd->bthd", probs, value, preferred_element_type=f32)
    return mixed.astype(bf16), top + jnp.log(totals)


def attend_backward(query, key, value, grads, logsum):
    scores = causal_scores(query, key)
    probs = jnp.exp(scores - logsum)
    value_grad = jnp.einsum("bhts,bthd->bsd", probs.astype(bf16), grads, preferred_element_type=f32)
    prob_grad = jnp.einsum("bthd,bsd->bhts", grads, value, preferred_element_type=f32)
    delta = jnp.sum(prob_grad * probs, axis=-1, keepdims=True)
    score_grad = (probs * (prob_grad - delta) * HEAD_SIZE ** (-0.5)).astype(bf16)
    query_grad = jnp.einsum("bhts,bsd->bthd", score_grad, key, preferred_element_type=f32)
    key_grad = jnp.einsum("bhts,bthd->bsd", score_grad, query, preferred_element_type=f32)
    return query_grad, key_grad, value_grad


def adamw(weight, grad, moment, second, rate, decay):
    moment = beta_one * moment + (1.0 - beta_one) * grad
    second = beta_two * second + (1.0 - beta_two) * grad * grad
    fix_one = 1.0 - beta_one**STEP
    fix_two = 1.0 - beta_two**STEP
    weight = weight - rate * (
        moment / fix_one / (jnp.sqrt(second / fix_two) + adam_epsilon) + decay * weight
    )
    return (moment, second, weight)


def chosen(order, pieces):
    low = jnp.where(order == 0, pieces[0], pieces[1])
    high = jnp.where(order == 2, pieces[2], pieces[3])
    return jnp.where(order < 2, low, high)


def adam_kernel(spans, place, p0, p1, p2, p3, weight, moment, second, m_out, s_out, w_out):
    pieces = (p0, p1, p2, p3)
    for column, at, width in spans:
        grads = []
        for j in range(GROUP):
            order = (j + GROUP - place[0]) % GROUP
            grads.append(chosen(order, [p[:, at : at + width].astype(f32) for p in pieces]))
        if width % 128:
            blocks = [(column, GROUP * width, jnp.concatenate(grads, axis=1))]
        else:
            blocks = [(column + j * width, width, grads[j]) for j in range(GROUP)]
        for start, size, grad in blocks:
            cols = slice(start, start + size)
            new = adamw(
                weight[:, cols], grad, moment[:, cols], second[:, cols], matrix_rate, matrix_decay
            )
            m_out[:, cols], s_out[:, cols], w_out[:, cols] = new


def adam_step(spans, place, pieces, weight, moment, second, tile):
    rows, columns = weight.shape
    wide = pl.BlockSpec((tile, columns), lambda i, place: (i, 0))
    narrow = pl.BlockSpec((tile, pieces[0].shape[1]), lambda i, place: (i, 0))
    shape = jax.ShapeDtypeStruct(weight.shape, f32)
    return pl.pallas_call(
        functools.partial(adam_kernel, spans),
        grid_spec=pltpu.PrefetchScalarGridSpec(
            num_scalar_prefetch=1,
            grid=(rows // tile,),
            in_specs=[narrow] * 4 + [wide] * 3,
            out_specs=[wide] * 3,
        ),
        out_shape=[shape] * 3,
        compiler_params=pltpu.CompilerParams(vmem_limit_bytes=48 * 1024 * 1024),
        cost_estimate=pl.CostEstimate(
            flops=12 * rows * columns, bytes_accessed=26 * rows * columns, transcendentals=0
        ),
    )(place.reshape(1), *pieces, weight, moment, second)


def body(
    tokens,
    cotangent,
    lengths,
    qkv_weight,
    qkv_moment,
    qkv_second,
    out_weight,
    out_moment,
    out_second,
    gateup_weight,
    gateup_moment,
    gateup_second,
    down_weight,
    down_moment,
    down_second,
    gains,
    gain_moment,
    gain_second,
):
    count = tokens.shape[0]
    rows = count * GROUP
    place = lax.axis_index("rep")
    inputs = tokens.astype(f32)
    positions = jnp.arange(count, dtype=jnp.int32)
    valid = (positions < lengths[0]).astype(f32)[:, None]
    result_grad = cotangent.astype(f32) * valid
    output_low = result_grad.astype(bf16)
    cosine_table, sine_table = rotary_tables(count)

    def cut(weight, start, width):
        return lax.dynamic_slice_in_dim(weight, start + place * width, width, axis=1).astype(bf16)

    qkv_part = jnp.concatenate(
        [
            cut(qkv_weight, 0, Q_COLS),
            cut(qkv_weight, WIDTH, KV_COLS),
            cut(qkv_weight, WIDTH + KV_WIDTH, KV_COLS),
        ],
        axis=1,
    )
    quarter = out_weight.shape[1] // GROUP
    out_rows = out_weight.shape[0]
    turned = turn(
        jnp.concatenate([cut(out_weight, 0, quarter), cut(down_weight, 0, quarter)], axis=0)
    )
    near = spread(jnp.concatenate([qkv_part, turned[:out_rows]], axis=1))
    qkv = near[:, : qkv_part.shape[1]]
    out = near[:, qkv_part.shape[1] :].reshape(GROUP, -1, quarter)
    gateup = spread(
        jnp.concatenate([cut(gateup_weight, 0, FF_COLS), cut(gateup_weight, FF, FF_COLS)], axis=1)
    )
    down = spread(turned[out_rows:]).reshape(GROUP, -1, quarter)

    both = gather_rows(jnp.concatenate([tokens, output_low], axis=1))
    group_inputs = both[:, :WIDTH].astype(f32)
    group_low = both[:, WIDTH:]

    group_inverse = norm_inverse(group_inputs)
    first_low = (group_inputs * group_inverse * gains[0]).astype(bf16)
    joined = dot(first_low, qkv, 1, 0)
    query = rotate_pairs(
        joined[:, :Q_COLS].reshape(GROUP, count, HEADS, HEAD_SIZE), cosine_table, sine_table
    ).astype(bf16)
    key = rotate_pairs(
        joined[:, Q_COLS : Q_COLS + KV_COLS].reshape(GROUP, count, 1, HEAD_SIZE),
        cosine_table,
        sine_table,
    ).astype(bf16)[:, :, 0]
    value = joined[:, Q_COLS + KV_COLS :].reshape(GROUP, count, HEAD_SIZE).astype(bf16)
    mixed, logsum = attend(query, key, value)
    mixed_low = mixed.reshape(rows, Q_COLS)
    branch = dot(mixed_low, out, 1, 1).reshape(rows, WIDTH)
    middle = inputs + scatter_rows(branch, count)
    second_inverse = norm_inverse(middle)
    second_low = gather_rows((middle * second_inverse * gains[1]).astype(bf16))
    wide = dot(second_low, gateup, 1, 0)
    gate = wide[:, :FF_COLS]
    up_part = wide[:, FF_COLS:]
    hidden_low = (jax.nn.silu(gate) * up_part).astype(bf16)
    output = dot(hidden_low, down, 1, 1).reshape(rows, WIDTH)
    block_output = ((middle + scatter_rows(output, count)) * valid).astype(bf16)

    hidden_grad = sum(
        dot(group_low[:, j * quarter : (j + 1) * quarter], down[j], 1, 1) for j in range(GROUP)
    )
    sigma = jax.nn.sigmoid(gate)
    gate_grad = hidden_grad * up_part * sigma * (1.0 + gate * (1.0 - sigma))
    up_grad = hidden_grad * jax.nn.silu(gate)
    wide_grad = jnp.concatenate([gate_grad, up_grad], axis=1).astype(bf16)
    second_grad = scatter_rows(dot(wide_grad, gateup, 1, 1), count)
    down_piece = collect_far(
        lax.dot_general(
            group_low.reshape(rows, GROUP, quarter),
            hidden_low,
            (((0,), (0,)), ((), ())),
            preferred_element_type=f32,
        ).transpose(0, 2, 1).reshape(GROUP * FF_COLS, quarter)
    )
    gateup_piece = collect_far(dot(second_low, wide_grad, 0, 0))
    second_gain_grad = jnp.sum(second_grad * middle * second_inverse, axis=0)
    middle_grad = result_grad + norm_backward(middle, second_inverse, gains[1], second_grad)
    branch_low = gather_rows(middle_grad.astype(bf16))

    mixed_grad = sum(
        dot(branch_low[:, j * quarter : (j + 1) * quarter], out[j], 1, 1) for j in range(GROUP)
    ).astype(bf16)
    out_terms = (
        lax.dot_general(
            branch_low.reshape(rows, GROUP, quarter),
            mixed_low,
            (((0,), (0,)), ((), ())),
            preferred_element_type=f32,
        ).transpose(0, 2, 1).reshape(GROUP * Q_COLS, quarter)
    )
    query_grad, key_grad, value_grad = attend_backward(
        query, key, value, mixed_grad.reshape(GROUP, count, HEADS, HEAD_SIZE), logsum
    )
    joined_grad = jnp.concatenate(
        [
            unrotate(query_grad, cosine_table, sine_table).reshape(rows, Q_COLS),
            unrotate(key_grad[:, :, None], cosine_table, sine_table).reshape(rows, KV_COLS),
            value_grad.reshape(rows, KV_COLS),
        ],
        axis=1,
    ).astype(bf16)
    qkv_terms = dot(first_low, joined_grad, 0, 0)
    first_partial = dot(joined_grad, qkv, 1, 1)
    first_gain_grad = jnp.sum(first_partial * group_inputs * group_inverse, axis=0)
    first_grad = scatter_rows(first_partial, count)
    input_grad = middle_grad + norm_backward(inputs, group_inverse[:count], gains[0], first_grad)
    gain_rows = qkv_weight.shape[0]
    gain_terms = jnp.stack([first_gain_grad, second_gain_grad]).reshape(gain_rows, -1)
    gain_terms = jnp.tile(gain_terms, (qkv_terms.shape[0] // gain_rows, 1))
    near_piece = collect(jnp.concatenate([qkv_terms, out_terms, gain_terms], axis=1), "fsdp_0")
    qkv_cols = qkv_terms.shape[1]
    out_piece = near_piece[:, qkv_cols : qkv_cols + quarter]
    qkv_pieces = share(
        jnp.concatenate([near_piece[:, :qkv_cols], near_piece[:, qkv_cols + quarter :]], axis=1)
    )
    gain_grad = sum(p[:, qkv_cols:].astype(f32) for p in qkv_pieces).reshape(gains.shape)

    qkv_spans = (
        (0, 0, Q_COLS),
        (WIDTH, Q_COLS, KV_COLS),
        (WIDTH + KV_WIDTH, Q_COLS + KV_COLS, KV_COLS),
    )
    down_new = adam_step(
        ((0, 0, quarter),), place, share_turned(down_piece), down_weight, down_moment, down_second, 88
    )
    gateup_new = adam_step(
        ((0, 0, FF_COLS), (FF, FF_COLS, FF_COLS)),
        place,
        share(gateup_piece),
        gateup_weight,
        gateup_moment,
        gateup_second,
        16,
    )
    out_new = adam_step(
        ((0, 0, quarter),), place, share_turned(out_piece), out_weight, out_moment, out_second, 32
    )
    qkv_new = adam_step(
        qkv_spans, place, qkv_pieces, qkv_weight, qkv_moment, qkv_second, 32
    )
    gain_new = adamw(gains, gain_grad, gain_moment, gain_second, gain_rate, 0.0)
    return (
        block_output,
        input_grad,
        *qkv_new,
        *out_new,
        *gateup_new,
        *down_new,
        *gain_new,
    )


def solution(mesh):
    finer = Mesh(
        mesh.devices.reshape(4, 4, 2, mesh.shape["rep"]), ("fsdp_0", "fsdp_1", "fsdp_2", "rep")
    )
    row = P(FSDP_REP, None)
    weight = P(FSDP, None)
    return jax.shard_map(
        body,
        mesh=finer,
        in_specs=(row, row, P(FSDP_REP)) + (weight,) * 12 + (P(),) * 3,
        out_specs=(row, row) + (weight,) * 12 + (P(),) * 3,
        check_vma=False,
    )
```

```python
import functools

import jax
import jax.numpy as jnp
from jax import lax
from jax.experimental import pallas as pl
from jax.experimental.pallas import tpu as pltpu
from jax.sharding import Mesh
from jax.sharding import PartitionSpec as P

QUERY_HEADS = 32
KEY_VALUE_HEADS = 4
HEAD = 64
FF = 5632
STEP = 10
GROUP = 4
WIDTH = QUERY_HEADS * HEAD
KV_WIDTH = KEY_VALUE_HEADS * HEAD
HEADS = QUERY_HEADS // GROUP
Q_COLS = WIDTH // GROUP
KV_COLS = KV_WIDTH // GROUP
QKV = Q_COLS + 2 * KV_COLS
NEAR = QKV + Q_COLS
MSG = NEAR + 128
FF_COLS = FF // GROUP
COUNT = 128
FSDP = ("fsdp_0", "fsdp_1", "fsdp_2")
FSDP_REP = ("fsdp_0", "fsdp_1", "fsdp_2", "rep")

EPS = 1e-05
beta_one = 0.9
beta_two = 0.999
adam_epsilon = 1e-08
matrix_rate = 0.02
matrix_decay = 0.1
gain_rate = 0.5
masked = -1e30
f32 = jnp.float32
bf16 = jnp.bfloat16
NT = (((1,), (1,)), ((), ()))
TN = (((0,), (0,)), ((), ()))
VMEM_LIMIT = 56 * 1024 * 1024

TURN = [(z * GROUP + x, x * GROUP + z) for z in range(GROUP) for x in range(GROUP)]


def fetch(block, k, axis="rep"):
    return lax.ppermute(block, axis, [((i + k) % GROUP, i) for i in range(GROUP)])


def send(block, k, axis="rep"):
    return lax.ppermute(block, axis, [(i, (i + k) % GROUP) for i in range(GROUP)])


def swap(block):
    return lax.ppermute(block, "fsdp_2", [(0, 1), (1, 0)])


def turn(piece):
    return lax.ppermute(piece, ("fsdp_0", "rep"), TURN)


def gather_rows(block):
    got = {k: fetch(block, k) for k in (2, 1, 3)}
    return [block, got[1], got[2], got[3]]


def hand_out(own, far1, far2, far3):
    return [own, send(far2, 2), send(far1, 1), send(far3, 3)]


def scatter_rows(*terms):
    return sum(g.astype(f32) for g in hand_out(*terms))


def share(piece):
    return [piece] + [fetch(piece, k) for k in range(1, GROUP)]


def send_line(parts, axis):
    return [parts[0], *(send(parts[k], k, axis) for k in (2, 1, 3))]


def total(terms):
    return sum(g.astype(f32) for g in terms)


def add_pair(kept, other):
    return (kept.astype(f32) + other.astype(f32)).astype(bf16)


def norm_inverse(values):
    return lax.rsqrt(jnp.mean(values * values, axis=-1, keepdims=True) + EPS)


def norm_backward(values, inverse, gain, grads):
    scaled = grads * gain
    return inverse * scaled - values * (inverse * inverse * inverse) * jnp.mean(
        scaled * values, axis=-1, keepdims=True
    )


def make_tables():
    positions=jnp.arange(COUNT,dtype=f32)
    freqs=jnp.power(10000.0,-(jnp.arange(0,HEAD,2,dtype=f32)/HEAD))
    ang=positions[:,None]*freqs[None,:]
    c,s,o=jnp.cos(ang),jnp.sin(ang),jnp.zeros_like(ang)
    i=jnp.ones_like(ang)
    q=lambda a,b: [a,b,a,b]
    return jnp.stack([jnp.concatenate([c,c,c,c,c,c,i,i],1),jnp.concatenate([-s,o,-s,o,-s,o,o,o],1),jnp.concatenate([o,s,o,s,o,s,o,o],1)])


def near_copies(near, qkv, out, sems):
    copies = [pltpu.make_async_copy(near.at[:, pl.ds(0, QKV)], qkv, sems.at[GROUP])]
    for z in range(GROUP):
        copies.append(
            pltpu.make_async_copy(
                near.at[pl.ds(z * Q_COLS, Q_COLS), pl.ds(QKV, Q_COLS)],
                out.at[:, pl.ds(z * Q_COLS, Q_COLS)],
                sems.at[z],
            )
        )
    return copies

def turned(u, tables, at):
    low, high = tables[1, :, at : at + 128], tables[2, :, at : at + 128]
    return pltpu.roll(u, 96, 1) * low + pltpu.roll(u, 32, 1) * high

def paired(block):
    lane = lax.broadcasted_iota(jnp.int32, block.shape, 1)
    zero = jnp.zeros_like(block)
    return jnp.concatenate([jnp.where(lane < 64, block, zero), jnp.where(lane < 64, zero, block)], axis=0)

def doubled(kv):
    lane = lax.broadcasted_iota(jnp.int32, kv.shape, 1)
    swapped = pltpu.roll(kv, 64, 1)
    return jnp.where(lane < 64, kv, swapped), jnp.where(lane < 64, swapped, kv)

def softmax_parts(query, keys):
    scores = lax.dot_general(query, keys, NT, preferred_element_type=f32) * HEAD ** (-0.5)
    row = lax.broadcasted_iota(jnp.int32, scores.shape, 0) % COUNT
    col = lax.broadcasted_iota(jnp.int32, scores.shape, 1) % COUNT
    scores = jnp.where(row >= col, scores, masked)
    parts = []
    for i in range(2):
        part = scores[:, i * COUNT : (i + 1) * COUNT]
        expos = jnp.exp(part - jnp.max(part, axis=-1, keepdims=True))
        parts.append(expos / jnp.sum(expos, axis=-1, keepdims=True))
    return parts

def stacked(ref, rows):
    return jnp.concatenate([ref[rows, p * 128 : (p + 1) * 128] for p in range(4)], axis=0)

def attend_kernel(p0, p1, p2, p3, gain, tables, near, own, far1, far2, far3, first, joined, mixed, qkv, out, wide, sems):
    copies = near_copies(near, qkv, out, sems)
    for c in copies: c.start()
    for k, p in enumerate((p0, p1, p2, p3)):
        x = p[...].astype(f32)
        inverse = lax.rsqrt(jnp.mean(x * x, axis=-1, keepdims=True) + EPS)
        first[k * COUNT : (k + 1) * COUNT, :] = (x * inverse * gain[...]).astype(bf16)
    for c in copies: c.wait()
    wide[...] = jnp.dot(first[...], qkv[...], preferred_element_type=f32)

    @pl.loop(0, 4)
    def _(k):
        rows = pl.ds(pl.multiple_of(k * COUNT, COUNT), COUNT)
        for p in range(5):
            cols = slice(p * 128, (p + 1) * 128)
            at = 0 if p < 4 else 128
            u = wide[rows, cols]
            joined[rows, cols] = (u * tables[0, :, at : at + 128] + turned(u, tables, at)).astype(bf16)
        key, value = doubled(joined[rows, Q_COLS:].astype(f32))
        probs = softmax_parts(stacked(joined, rows), paired(key.astype(bf16)))
        probs = jnp.concatenate([p.astype(bf16) for p in probs], axis=1)
        got = jnp.dot(probs, paired(value.astype(bf16)), preferred_element_type=f32).astype(bf16)
        for p in range(4):
            mixed[rows, p * 128 : (p + 1) * 128] = got[p * COUNT : (p + 1) * COUNT]

    @pl.loop(0, WIDTH // 512)
    def _(n):
        cols = pl.ds(pl.multiple_of(n * 512, 512), 512)
        part = jnp.dot(mixed[...], out[:, cols], preferred_element_type=f32)
        own[:, cols] = part[:COUNT]
        for k, far in ((1, far1), (2, far2), (3, far3)):
            far[:, cols] = part[k * COUNT : (k + 1) * COUNT].astype(bf16)

def attend_group(pieces, gain, tables, near):
    any_=pl.BlockSpec(memory_space=pl.ANY); vm=pl.BlockSpec(memory_space=pltpu.VMEM)
    sd=jax.ShapeDtypeStruct; n=4*COUNT
    return pl.pallas_call(attend_kernel,in_specs=[vm]*6+[any_],out_specs=[vm]*7,
        out_shape=[sd((COUNT,WIDTH),f32)]+[sd((COUNT,WIDTH),bf16)]*3+[sd((n,WIDTH),bf16),sd((n,QKV),bf16),sd((n,Q_COLS),bf16)],
        scratch_shapes=[pltpu.VMEM((WIDTH,QKV),bf16),pltpu.VMEM((Q_COLS,WIDTH),bf16),pltpu.VMEM((n,QKV),f32),pltpu.SemaphoreType.DMA((GROUP + 1,))],
        compiler_params=pltpu.CompilerParams(vmem_limit_bytes=VMEM_LIMIT),
        cost_estimate=pl.CostEstimate(flops=2*n*WIDTH*NEAR*2,bytes_accessed=2*(2*WIDTH*NEAR+3*n*WIDTH),transcendentals=n*HEADS*COUNT),
    )(*pieces,gain,tables,near)

def attend_back_kernel(place, d0, d1, d2, d3, p0, p1, p2, p3, second_gain, tables, near, first, joined, mixed,
                       own, far1, far2, far3, message_a, kept_a, message_b, kept_b, qkv, out, grads, mixed_grad, joined_grad, first_turned, mixed_turned, extra, sems):
    copies = near_copies(near, qkv, out, sems)
    for c in copies: c.start()
    z, y, core = place[0], place[1], place[2]
    for k, d in enumerate((d0, d1, d2, d3)):
        grads[k * COUNT : (k + 1) * COUNT, :] = d[...]
    inverses = []
    for p in (p0, p1, p2, p3):
        x = p[...].astype(f32)
        inverses.append(lax.rsqrt(jnp.mean(x * x, axis=-1, keepdims=True) + EPS))
    extra[...] = jnp.zeros_like(extra)
    for i in range(16):
        extra[16 + i : 17 + i, :] = second_gain[:, i * 128 : (i + 1) * 128]
    for c in copies: c.wait()
    mixed_grad[...] = lax.dot_general(grads[...], out[...], NT, preferred_element_type=f32).astype(bf16)

    @pl.loop(0, 4)
    def _(k):
        rows = pl.ds(pl.multiple_of(k * COUNT, COUNT), COUNT)
        key, value = doubled(joined[rows, Q_COLS:].astype(f32))
        keys, values = paired(key.astype(bf16)), paired(value.astype(bf16))
        query = stacked(joined, rows)
        upper = stacked(mixed_grad, rows)
        probs = softmax_parts(query, keys)
        prob_grad = lax.dot_general(upper, values, NT, preferred_element_type=f32)
        score_grad = []
        for i in range(2):
            part = prob_grad[:, i * COUNT : (i + 1) * COUNT]
            delta = jnp.sum(part * probs[i], axis=-1, keepdims=True)
            score_grad.append((probs[i] * (part - delta) * HEAD ** (-0.5)).astype(bf16))
        score_grad = jnp.concatenate(score_grad, axis=1)
        probs = jnp.concatenate([p.astype(bf16) for p in probs], axis=1)
        query_grad = jnp.dot(score_grad, keys, preferred_element_type=f32)
        key_grad = lax.dot_general(score_grad, query, TN, preferred_element_type=f32)
        value_grad = lax.dot_general(probs, upper, TN, preferred_element_type=f32)
        lane = lax.broadcasted_iota(jnp.int32, (COUNT, 128), 1)
        key_grad = key_grad[:COUNT] + pltpu.roll(key_grad[COUNT:], 64, 1)
        value_grad = pltpu.roll(value_grad[:COUNT], 64, 1) + value_grad[COUNT:]
        both = jnp.where(lane < 64, key_grad, value_grad)
        for p in range(5):
            at = 0 if p < 4 else 128
            w = query_grad[p * COUNT : (p + 1) * COUNT] if p < 4 else both
            joined_grad[rows, p * 128 : (p + 1) * 128] = (w * tables[0, :, at : at + 128] - turned(w, tables, at)).astype(bf16)

    @pl.loop(0, WIDTH // 512)
    def _(n):
        cols = pl.ds(pl.multiple_of(n * 512, 512), 512)
        part = lax.dot_general(joined_grad[...], qkv[cols, :], NT, preferred_element_type=f32)
        own[:, cols] = part[:COUNT]
        for k, far in ((1, far1), (2, far2), (3, far3)):
            far[:, cols] = part[k * COUNT : (k + 1) * COUNT].astype(bf16)
        total = jnp.zeros((1, 512), f32)
        for k, p in enumerate((p0, p1, p2, p3)):
            scaled = p[:, cols].astype(f32) * inverses[k]
            total = total + jnp.sum(part[k * COUNT : (k + 1) * COUNT] * scaled, axis=0, keepdims=True)
        for i in range(4):
            extra[pl.ds(n * 4 + i, 1), :] = total[:, i * 128 : (i + 1) * 128]

    for k in range(4):
        rows = slice(k * COUNT, (k + 1) * COUNT)
        first_turned[:, rows] = first[rows, :].T
        mixed_turned[:, rows] = mixed[rows, :].T

    @pl.loop(0, 4)
    def _(zi):
        dz = (zi + 4 - z) % 4
        rows = pl.ds(pl.multiple_of(zi * 512, 512), 512)
        left = jnp.dot(first_turned[rows, :], joined_grad[...], preferred_element_type=f32).astype(bf16)
        right = jnp.dot(mixed_turned[...], grads[:, rows], preferred_element_type=f32).astype(bf16)
        for yi in range(4):
            dy = (yi + 4 - y) % 4
            for owner in range(2):
                at = slice((yi * 2 + owner) * 64, (yi * 2 + owner + 1) * 64)
                def store(ref_a, ref_b):
                    ref_a[dz, dy, :, :QKV] = left[at]
                    ref_a[dz, dy, :, QKV:] = extra[...].astype(bf16)
                    ref_b[dy, dz] = right[at]
                @pl.when(core == owner)
                def _():
                    store(kept_a, kept_b)
                @pl.when(core != owner)
                def _():
                    store(message_a, message_b)

def attend_back_group(place, grads, pieces, second_gain, tables, near, first, joined, mixed):
    any_=pl.BlockSpec(memory_space=pl.ANY); vm=pl.BlockSpec(memory_space=pltpu.VMEM); sm=pl.BlockSpec(memory_space=pltpu.SMEM)
    sd=jax.ShapeDtypeStruct; n=4*COUNT
    return pl.pallas_call(attend_back_kernel,in_specs=[sm]+[vm]*10+[any_]+[vm]*3,out_specs=[vm]*8,
        out_shape=[sd((COUNT,WIDTH),f32)]+[sd((COUNT,WIDTH),bf16)]*3+[sd((4,4,64,QKV+128),bf16)]*2+[sd((4,4,64,Q_COLS),bf16)]*2,
        scratch_shapes=[pltpu.VMEM((WIDTH,QKV),bf16),pltpu.VMEM((Q_COLS,WIDTH),bf16),pltpu.VMEM((n,WIDTH),bf16),pltpu.VMEM((n,Q_COLS),bf16),pltpu.VMEM((n,QKV),bf16),
            pltpu.VMEM((WIDTH,n),bf16),pltpu.VMEM((Q_COLS,n),bf16),pltpu.VMEM((64,128),f32),pltpu.SemaphoreType.DMA((GROUP + 1,))],
        compiler_params=pltpu.CompilerParams(vmem_limit_bytes=VMEM_LIMIT),
        cost_estimate=pl.CostEstimate(flops=2*n*WIDTH*NEAR*3,bytes_accessed=2*(4*WIDTH*NEAR+6*n*WIDTH),transcendentals=n*HEADS*COUNT),
    )(place,*grads,*pieces,second_gain,tables,near,first,joined,mixed)

def ffn_kernel(order, p0, p1, p2, p3, d0, d1, d2, d3, weights, terms, hidden, wide_grad, rows, turned, gateup, down, wide, row_sem, grad_sem, gateup_sem, down_sem):
    count = p0.shape[0]
    blocks, depth = gateup.shape[0] // 64, 64
    lanes = 128
    row_copies = [pltpu.make_async_copy(p, rows.at[pl.ds(k * count, count)], row_sem.at[k]) for k, p in enumerate((p0, p1, p2, p3))]
    for c in row_copies: c.start()
    def gateup_copy(t):
        return pltpu.make_async_copy(
            weights.at[:, pl.ds(t * depth, depth), :],
            gateup.reshape(blocks, depth, 2 * FF_COLS).at[:, :, pl.ds(pl.multiple_of(t * lanes, lanes), lanes)],
            gateup_sem.at[t])
    tiles = 2 * FF_COLS // lanes
    for t in range(tiles): gateup_copy(t).start()
    grad_copies = [
        pltpu.make_async_copy(d, turned.at[pl.ds(k * count, count)], grad_sem.at[k])
        for k, d in enumerate((d0, d1, d2, d3))
    ]
    for c in grad_copies:
        c.start()
    down_rows = FF_COLS // 8
    def down_copy(z, ct):
        return pltpu.make_async_copy(
            weights.at[pl.ds(z * 8, 8), pl.ds(tiles * depth + ct * down_rows, down_rows), :],
            down.reshape(8, down_rows, WIDTH).at[:, :, pl.ds((z * 4 + ct) * lanes, lanes)],
            down_sem.at[z * 4 + ct])
    for z in range(4):
        for ct in range(4): down_copy(z, ct).start()
    for c in row_copies: c.wait()

    @pl.loop(0, 2 * FF_COLS // 256)
    def _(t):
        gateup_copy(2 * t).wait()
        gateup_copy(2 * t + 1).wait()
        cols = pl.ds(pl.multiple_of(t * 256, 256), 256)
        wide[:, cols] = jnp.dot(rows[...], gateup[:, cols], preferred_element_type=f32)

    for c in grad_copies:
        c.wait()
    for z in range(4):
        for ct in range(4): down_copy(z, ct).wait()

    def back(start, width):
        cols = pl.ds(start, width)
        ups = pl.ds(pl.multiple_of(FF_COLS + start, 128), width)
        hidden_grad = lax.dot_general(turned[...], down[cols, :], NT, preferred_element_type=f32)
        gate = wide[:, cols]
        up_part = wide[:, ups]
        sigma = 1.0 / (1.0 + jnp.exp(-gate))
        act = gate * sigma
        hidden[:, cols] = (act * up_part).astype(bf16)
        wide_grad[:, cols] = (hidden_grad * up_part * sigma * (1.0 + gate * (1.0 - sigma))).astype(bf16)
        wide_grad[:, ups] = (hidden_grad * act).astype(bf16)

    @pl.loop(0, FF_COLS // 256)
    def _(t):
        back(pl.multiple_of(t * 256, 256), 256)
    if FF_COLS % 256:
        back(FF_COLS // 256 * 256, FF_COLS % 256)

    @pl.loop(0, WIDTH // 256)
    def _(n):
        cols = pl.ds(pl.multiple_of(n * 256, 256), 256)
        part = lax.dot_general(wide_grad[...], gateup[cols, :], NT, preferred_element_type=f32)
        part = part.astype(bf16)
        for k in range(GROUP):
            terms[(order[0] + k) % GROUP, :, cols] = part[k * count : (k + 1) * count]


def ffn(order, pieces, grads, weights):
    count=pieces[0].shape[0]; n=4*count
    any_=pl.BlockSpec(memory_space=pl.ANY); vm=pl.BlockSpec(memory_space=pltpu.VMEM)
    sd=jax.ShapeDtypeStruct
    tiles=2*FF_COLS//128
    return pl.pallas_call(
        ffn_kernel,
        in_specs=[pl.BlockSpec(memory_space=pltpu.SMEM)]+[any_]*9, out_specs=[vm]*3,
        out_shape=[sd((GROUP,count,WIDTH),bf16),sd((n,FF_COLS),bf16),sd((n,2*FF_COLS),bf16)],
        scratch_shapes=[pltpu.VMEM((n,WIDTH),bf16),pltpu.VMEM((n,WIDTH),bf16),pltpu.VMEM((WIDTH,2*FF_COLS),bf16),pltpu.VMEM((FF_COLS,WIDTH),bf16),pltpu.VMEM((n,2*FF_COLS),f32),
            pltpu.SemaphoreType.DMA((4,)),pltpu.SemaphoreType.DMA((4,)),pltpu.SemaphoreType.DMA((tiles,)),pltpu.SemaphoreType.DMA((16,))],
        compiler_params=pltpu.CompilerParams(vmem_limit_bytes=VMEM_LIMIT),
        cost_estimate=pl.CostEstimate(flops=2*n*WIDTH*FF_COLS*5,bytes_accessed=2*(3*WIDTH*FF_COLS+3*n*WIDTH+3*n*FF_COLS),transcendentals=n*FF_COLS),
    )(order.reshape(1),*pieces,*grads,weights)

def ffn_terms_kernel(place, *refs):
    own, refs = refs[:4], refs[4:]
    near, refs = refs[:4], refs[4:]
    grad_refs, refs = refs[:4], refs[4:]
    other_grads, hidden_refs, wide_refs, out = refs[0], refs[1:3], refs[3:5], refs[5]
    rows, turned, raw, grads, hidden, wide, tiles, blocks, in_sem, out_sem = refs[6:]
    core = place[2]
    span = 4 * COUNT
    depth = FF_COLS // 8
    steps = 2 * FF_COLS // 256
    row_loads = [
        pltpu.make_async_copy(p, raw.at[pl.ds(k * COUNT, COUNT)], in_sem.at[k])
        for k, p in enumerate((*own, *near))
    ]
    wide_loads = [
        pltpu.make_async_copy(w, wide.at[pl.ds(i * span, span)], in_sem.at[8 + i])
        for i, w in enumerate(wide_refs)
    ]
    late_loads = [
        pltpu.make_async_copy(w, hidden.at[pl.ds(i * span, span)], in_sem.at[10 + i])
        for i, w in enumerate(hidden_refs)
    ]
    late_loads += [
        pltpu.make_async_copy(d, grads.at[pl.ds(k * COUNT, COUNT)], in_sem.at[12 + k])
        for k, d in enumerate(grad_refs)
    ]
    late_loads.append(pltpu.make_async_copy(other_grads, grads.at[pl.ds(span, span)], in_sem.at[16]))
    for c in (*row_loads, *wide_loads, *late_loads):
        c.start()
    for k, c in enumerate(row_loads):
        c.wait()
        cols = slice(k * COUNT, (k + 1) * COUNT)
        both = raw[cols, :].T.reshape(16, 2, 64, COUNT)
        rows[:, cols] = jnp.where(core == 0, both[:, 0], both[:, 1]).reshape(WIDTH // 2, COUNT)
    for c in wide_loads:
        c.wait()

    def tile_store(t):
        return pltpu.make_async_copy(
            tiles.at[t % 2],
            out.at[:, pl.ds(pl.multiple_of(t * 128, 128), 128), :],
            out_sem.at[t % 2],
        )

    @pl.loop(0, steps)
    def _(t):
        @pl.when(t >= 2)
        def _():
            tile_store(t - 2).wait()

        cols = pl.ds(pl.multiple_of(t * 256, 256), 256)
        part = jnp.dot(rows[...], wide[:, cols], preferred_element_type=f32).astype(bf16)
        part = part.reshape(16, 64, 256)
        for i in range(2):
            tiles[t % 2, :, i * 64 : (i + 1) * 64, :] = part[:, :, i * 128 : (i + 1) * 128]
        tile_store(t).start()

    for c in late_loads:
        c.wait()
    for k in range(8):
        cols = slice(k * COUNT, (k + 1) * COUNT)
        both = hidden[cols, :].T.reshape(GROUP, 2, depth, COUNT)
        turned[:, cols] = jnp.where(core == 0, both[:, 0], both[:, 1]).reshape(FF_COLS // 2, COUNT)

    def block_store(t):
        return pltpu.make_async_copy(
            blocks.at[t % 2],
            out.at[
                pl.ds(t // 2 * GROUP, GROUP),
                pl.ds(pl.multiple_of(FF_COLS + t % 2 * 2 * depth, 32), 2 * depth),
                :,
            ],
            out_sem.at[2 + t % 2],
        )

    @pl.loop(0, 8)
    def _(t):
        @pl.when(t >= 2)
        def _():
            block_store(t - 2).wait()

        cols = pl.ds(pl.multiple_of(t * 256, 256), 256)
        part = jnp.dot(turned[...], grads[:, cols], preferred_element_type=f32).astype(bf16)
        part = part.reshape(GROUP, depth, 256)
        for i in range(2):
            blocks[t % 2, :, i * depth : (i + 1) * depth, :] = part[:, :, i * 128 : (i + 1) * 128]
        block_store(t).start()

    tile_store(steps - 2).wait()
    tile_store(steps - 1).wait()
    block_store(6).wait()
    block_store(7).wait()


def ffn_terms(place, pieces, other_pieces, grads, other_grads, hidden, other_hidden, wide, other_wide):
    n = 8 * COUNT
    any_ = pl.BlockSpec(memory_space=pl.ANY)
    return pl.pallas_call(
        ffn_terms_kernel,
        in_specs=[pl.BlockSpec(memory_space=pltpu.SMEM)] + [any_] * 17,
        out_specs=any_,
        out_shape=jax.ShapeDtypeStruct((16, 2112, 128), bf16),
        scratch_shapes=[
            pltpu.VMEM((WIDTH // 2, n), bf16),
            pltpu.VMEM((FF_COLS // 2, n), bf16),
            pltpu.VMEM((n, WIDTH), bf16),
            pltpu.VMEM((n, WIDTH), bf16),
            pltpu.VMEM((n, FF_COLS), bf16),
            pltpu.VMEM((n, 2 * FF_COLS), bf16),
            pltpu.VMEM((2, 16, 128, 128), bf16),
            pltpu.VMEM((2, GROUP, FF_COLS // 4, 128), bf16),
            pltpu.SemaphoreType.DMA((17,)),
            pltpu.SemaphoreType.DMA((4,)),
        ],
        compiler_params=pltpu.CompilerParams(vmem_limit_bytes=VMEM_LIMIT),
        cost_estimate=pl.CostEstimate(
            flops=3 * n * WIDTH * FF_COLS,
            bytes_accessed=3 * WIDTH * FF_COLS + 4 * n * WIDTH + 6 * n * FF_COLS,
            transcendentals=0,
        ),
    )(place, *pieces, *other_pieces, *grads, other_grads, hidden, other_hidden, wide, other_wide)


def ffn_out_kernel(hidden, weights, own, far1, far2, far3, down, down_sem):
    count=own.shape[0]
    depth = 64
    tiles = 2 * FF_COLS // 128
    down_rows = FF_COLS // 8
    def down_copy(z, ct):
        return pltpu.make_async_copy(
            weights.at[pl.ds(z * 8, 8), pl.ds(tiles * depth + ct * down_rows, down_rows), :],
            down.reshape(8, down_rows, WIDTH).at[:, :, pl.ds((z * 4 + ct) * 128, 128)],
            down_sem.at[z * 4 + ct])
    for z in range(4):
        for ct in range(4): down_copy(z, ct).start()
    for z in range(4):
        for ct in range(4): down_copy(z, ct).wait()
        cols = slice(z * 512, (z + 1) * 512)
        part = jnp.dot(hidden[...], down[:, cols], preferred_element_type=f32)
        own[:, cols] = part[:count]
        for k, far in ((1, far1), (2, far2), (3, far3)):
            far[:, cols] = part[k * count : (k + 1) * count].astype(bf16)
def ffn_out(hidden, weights):
    n=hidden.shape[0]; count=n//4
    any_=pl.BlockSpec(memory_space=pl.ANY); vm=pl.BlockSpec(memory_space=pltpu.VMEM)
    sd=jax.ShapeDtypeStruct
    return pl.pallas_call(ffn_out_kernel,in_specs=[vm,any_],out_specs=[vm]*4,
        out_shape=[sd((count,WIDTH),f32)]+[sd((count,WIDTH),bf16)]*3,
        scratch_shapes=[pltpu.VMEM((FF_COLS,WIDTH),bf16),pltpu.SemaphoreType.DMA((16,))],
        compiler_params=pltpu.CompilerParams(vmem_limit_bytes=VMEM_LIMIT),
        cost_estimate=pl.CostEstimate(flops=2*n*WIDTH*FF_COLS,bytes_accessed=2*(WIDTH*FF_COLS+n*WIDTH+n*FF_COLS),transcendentals=0),
    )(hidden,weights)
def adamw(weight, grad, moment, second, rate, decay):
    moment = beta_one * moment + (1.0 - beta_one) * grad
    second = beta_two * second + (1.0 - beta_two) * grad * grad
    scale_one = 1.0 / (1.0 - beta_one**STEP)
    scale_two = 1.0 / (1.0 - beta_two**STEP)
    weight = weight - rate * (
        moment * scale_one / (jnp.sqrt(second * scale_two) + adam_epsilon) + decay * weight
    )
    return (moment, second, weight)


def chosen(order, pieces):
    low = jnp.where(order == 0, pieces[0], pieces[1])
    high = jnp.where(order == 2, pieces[2], pieces[3])
    return jnp.where(order < 2, low, high)


def adam_gathered_kernel(piece, weight, moment, second, m_out, s_out, w_out):
    rows = weight.shape[0]
    for t in range(weight.shape[1] // 128):
        cols = slice(t * 128, (t + 1) * 128)
        m_out[:, cols], s_out[:, cols], w_out[:, cols] = adamw(
            weight[:, cols],
            piece[0, t * rows : (t + 1) * rows, :].astype(f32),
            moment[:, cols],
            second[:, cols],
            matrix_rate,
            matrix_decay,
        )


def adam_gathered(gathered, parts, weight, moment, second):
    rows, columns = weight.shape
    width = columns // (parts * GROUP)
    wide = pl.BlockSpec((rows, width), lambda p, j: (0, p * GROUP + j))
    piece = pl.BlockSpec((1, width // 128 * rows, 128), lambda p, j: (j, p, 0))
    return pl.pallas_call(
        adam_gathered_kernel,
        grid=(parts, GROUP),
        in_specs=[piece] + [wide] * 3,
        out_specs=[wide] * 3,
        out_shape=[jax.ShapeDtypeStruct(weight.shape, f32)] * 3,
        compiler_params=pltpu.CompilerParams(vmem_limit_bytes=VMEM_LIMIT),
        cost_estimate=pl.CostEstimate(
            flops=12 * rows * columns, bytes_accessed=26 * rows * columns, transcendentals=0
        ),
    )(gathered, weight, moment, second)


def adam_near_kernel(order, p0, p1, p2, p3, *refs):
    qkv, out, down = refs[0:3], refs[3:6], refs[6:9]
    qkv_new, out_new, down_new = refs[9:12], refs[12:15], refs[15:18]
    pieces = (p0, p1, p2, p3)
    depth, down_depth = qkv[0].shape[0], down[0].shape[0]
    last = Q_COLS // 128

    def step(old, new, start, grad):
        cols = pl.ds(start, grad.shape[1])
        new[0][:, cols], new[1][:, cols], new[2][:, cols] = adamw(
            old[0][:, cols], grad, old[1][:, cols], old[2][:, cols], matrix_rate, matrix_decay
        )

    down_at = (last + 2) * depth
    out_at = down_at + last * down_depth
    for k, p in enumerate(pieces):
        place = pl.multiple_of((order[0] + k) % GROUP * Q_COLS, 128)
        for t in range(last):
            for old, new, at, rows in (
                (down, down_new, down_at, down_depth),
                (qkv, qkv_new, 0, depth),
                (out, out_new, out_at, depth),
            ):
                grad = p[at + t * rows : at + (t + 1) * rows, :].astype(f32)
                step(old, new, pl.multiple_of(place + t * 128, 128), grad)
    both = []
    for j in range(GROUP):
        which = (j + GROUP - order[0]) % GROUP
        at = slice(last * depth, (last + 1) * depth)
        both.append(chosen(which, [p[at, :].astype(f32) for p in pieces]))
    step(qkv, qkv_new, WIDTH, jnp.concatenate([b[:, :KV_COLS] for b in both], axis=1))
    step(qkv, qkv_new, WIDTH + KV_WIDTH, jnp.concatenate([b[:, KV_COLS:] for b in both], axis=1))


def adam_near(order, pieces, *states):
    vm = pl.BlockSpec(memory_space=pltpu.VMEM)
    size = sum(a.size for a in states)
    return pl.pallas_call(
        adam_near_kernel,
        in_specs=[pl.BlockSpec(memory_space=pltpu.SMEM)] + [vm] * 13,
        out_specs=[vm] * 9,
        out_shape=[jax.ShapeDtypeStruct(a.shape, f32) for a in states],
        compiler_params=pltpu.CompilerParams(vmem_limit_bytes=VMEM_LIMIT),
        cost_estimate=pl.CostEstimate(flops=4 * size, bytes_accessed=9 * size, transcendentals=0),
    )(order.reshape(1), *pieces, *states)


def in_tiles(block):
    rows, columns = block.shape
    return block.reshape(rows, columns // 128, 128).transpose(1, 0, 2).reshape(-1, 128)


def body(
    tokens,
    cotangent,
    lengths,
    qkv_weight,
    qkv_moment,
    qkv_second,
    out_weight,
    out_moment,
    out_second,
    gateup_weight,
    gateup_moment,
    gateup_second,
    down_weight,
    down_moment,
    down_second,
    gains,
    gain_moment,
    gain_second,
):
    order = lax.axis_index("rep")
    spot = jnp.stack([lax.axis_index(a) for a in FSDP]).astype(jnp.int32)
    inputs = tokens.astype(f32)
    positions = jnp.arange(COUNT, dtype=jnp.int32)
    valid = (positions < lengths[0]).astype(f32)[:, None]
    result_grad = cotangent.astype(f32) * valid
    output_low = result_grad.astype(bf16)
    tables = make_tables()

    def cut(weight, start, width):
        return lax.dynamic_slice_in_dim(weight, start + order * width, width, axis=1).astype(bf16)

    quarter = WIDTH // GROUP
    down_rows = down_weight.shape[0]
    near_block = jnp.concatenate(
        [
            cut(qkv_weight, 0, Q_COLS),
            cut(qkv_weight, WIDTH, KV_COLS),
            cut(qkv_weight, WIDTH + KV_WIDTH, KV_COLS),
            turn(cut(out_weight, 0, quarter)),
        ],
        axis=1,
    )
    near = lax.all_gather(near_block, FSDP, axis=0, tiled=True)
    pieces = gather_rows(tokens)
    pieces, output_low = lax.optimization_barrier((pieces, output_low))
    group_grads = gather_rows(output_low)
    far_block = jnp.concatenate(
        [
            in_tiles(cut(gateup_weight, 0, FF_COLS)),
            in_tiles(cut(gateup_weight, FF, FF_COLS)),
            in_tiles(turn(cut(down_weight, 0, quarter))),
        ]
    )
    near, far_block, pieces, group_grads = lax.optimization_barrier(
        (near, far_block, pieces, group_grads)
    )
    far = lax.all_gather(far_block, FSDP, axis=0)

    *branch, first, joined, mixed = attend_group(pieces, gains[:1], tables, near)
    middle = inputs + scatter_rows(*branch)
    second_inverse = norm_inverse(middle)
    second = gather_rows((middle * second_inverse * gains[1]).astype(bf16))
    other_grads = swap(jnp.concatenate(group_grads))
    other_second = [swap(p) for p in second]
    second, other_second, other_grads = lax.optimization_barrier(
        (second, other_second, other_grads)
    )
    second_terms, hidden, wide_grad = ffn(order, second, group_grads, far)
    second_grad = lax.psum_scatter(
        second_terms.reshape(-1, WIDTH), "rep", scatter_dimension=0, tiled=True
    ).astype(f32)
    other_hidden, other_wide = swap(hidden), swap(wide_grad)
    far_terms = ffn_terms(
        spot, second, other_second, group_grads, other_grads, hidden, other_hidden, wide_grad, other_wide
    )
    far_piece = lax.psum_scatter(
        far_terms.reshape(-1, 128), FSDP[:2], scatter_dimension=0, tiled=True
    )
    second_gain_grad = jnp.sum(second_grad * middle * second_inverse, axis=0, keepdims=True)
    middle_grad = result_grad + norm_backward(middle, second_inverse, gains[1], second_grad)
    branch_low, hidden = lax.optimization_barrier((middle_grad.astype(bf16), hidden))
    branch_grads = gather_rows(branch_low)
    output_terms = ffn_out(hidden, far)
    branch_grads, output_terms = lax.optimization_barrier((branch_grads, output_terms))
    output = scatter_rows(*output_terms)

    *first_terms, message_a, kept_a, message_b, kept_b = attend_back_group(
        spot, branch_grads, pieces, second_gain_grad, tables, near, first, joined, mixed
    )
    message_a, message_b, output = lax.optimization_barrier((message_a, message_b, output))
    block_output = ((middle + output) * valid).astype(bf16)
    other_a, other_b = swap(message_a), swap(message_b)
    first_terms = hand_out(*first_terms)
    terms_a = send_line(add_pair(kept_a, other_a), "fsdp_0")
    terms_b = send_line(add_pair(kept_b, other_b), "fsdp_1")
    first_terms, terms_a, terms_b, far_piece = lax.optimization_barrier(
        (first_terms, terms_a, terms_b, far_piece)
    )
    wide_pieces = lax.all_gather(far_piece, "rep")
    terms_a = send_line(total(terms_a).astype(bf16), "fsdp_1")
    terms_b = send_line(total(terms_b).astype(bf16), "fsdp_0")
    tiles_a = in_tiles(total(terms_a).astype(bf16))
    tiles_b = in_tiles(total(terms_b).astype(bf16))
    depth = gateup_weight.shape[0]
    wide_rows = 2 * FF_COLS // 128 * depth
    away = turn(jnp.concatenate([far_piece[wide_rows:], tiles_b]))
    away, wide_pieces = lax.optimization_barrier((away, wide_pieces))
    near_pieces = share(jnp.concatenate([tiles_a, away]))
    gateup_new = adam_gathered(wide_pieces, 2, gateup_weight, gateup_moment, gateup_second)
    near_new = adam_near(
        order,
        near_pieces,
        qkv_weight,
        qkv_moment,
        qkv_second,
        out_weight,
        out_moment,
        out_second,
        down_weight,
        down_moment,
        down_second,
    )
    qkv_new, out_new, down_new = near_new[0:3], near_new[3:6], near_new[6:9]
    gain_at = QKV // 128 * depth
    gain_grad = sum(p[gain_at : gain_at + 2 * WIDTH // 128].astype(f32) for p in near_pieces)
    first_grad = total(first_terms)
    input_grad = middle_grad + norm_backward(inputs, norm_inverse(inputs), gains[0], first_grad)
    gain_new = adamw(gains, gain_grad.reshape(gains.shape), gain_moment, gain_second, gain_rate, 0.0)
    return (
        block_output,
        input_grad,
        *qkv_new,
        *out_new,
        *gateup_new,
        *down_new,
        *gain_new,
    )


def solution(mesh):
    finer = Mesh(
        mesh.devices.reshape(4, 4, 2, mesh.shape["rep"]), ("fsdp_0", "fsdp_1", "fsdp_2", "rep")
    )
    row = P(FSDP_REP, None)
    weight = P(FSDP, None)
    return jax.shard_map(
        body,
        mesh=finer,
        in_specs=(row, row, P(FSDP_REP)) + (weight,) * 12 + (P(),) * 3,
        out_specs=(row, row) + (weight,) * 12 + (P(),) * 3,
        check_vma=False,
    )
```

```python
import functools

import jax
import jax.numpy as jnp
from jax import lax
from jax.experimental import pallas as pl
from jax.experimental.pallas import tpu as pltpu
from jax.sharding import Mesh
from jax.sharding import PartitionSpec as P

QUERY_HEADS = 32
KEY_VALUE_HEADS = 4
HEAD = 64
FF = 5632
STEP = 10
GROUP = 4
WIDTH = QUERY_HEADS * HEAD
KV_WIDTH = KEY_VALUE_HEADS * HEAD
HEADS = QUERY_HEADS // GROUP
Q_COLS = WIDTH // GROUP
KV_COLS = KV_WIDTH // GROUP
QKV = Q_COLS + 2 * KV_COLS
NEAR = QKV + Q_COLS
MSG = NEAR + 128
FF_COLS = FF // GROUP
COUNT = 128
FSDP = ("fsdp_0", "fsdp_1", "fsdp_2")
FSDP_REP = ("fsdp_0", "fsdp_1", "fsdp_2", "rep")

EPS = 1e-05
beta_one = 0.9
beta_two = 0.999
adam_epsilon = 1e-08
matrix_rate = 0.02
matrix_decay = 0.1
gain_rate = 0.5
masked = -1e30
f32 = jnp.float32
bf16 = jnp.bfloat16
NT = (((1,), (1,)), ((), ()))
TN = (((0,), (0,)), ((), ()))
VMEM_LIMIT = 56 * 1024 * 1024

TURN = [(z * GROUP + x, x * GROUP + z) for z in range(GROUP) for x in range(GROUP)]


def fetch(block, k, axis="rep"):
    return lax.ppermute(block, axis, [((i + k) % GROUP, i) for i in range(GROUP)])


def send(block, k, axis="rep"):
    return lax.ppermute(block, axis, [(i, (i + k) % GROUP) for i in range(GROUP)])


def swap(block):
    return lax.ppermute(block, "fsdp_2", [(0, 1), (1, 0)])


def turn(piece):
    return lax.ppermute(piece, ("fsdp_0", "rep"), TURN)


def gather_rows(block):
    got = {k: fetch(block, k) for k in (2, 1, 3)}
    return [block, got[1], got[2], got[3]]


def hand_out(own, far1, far2, far3):
    return [own, send(far2, 2), send(far1, 1), send(far3, 3)]


def scatter_rows(*terms):
    return sum(g.astype(f32) for g in hand_out(*terms))


def share(piece):
    return [piece] + [fetch(piece, k) for k in range(1, GROUP)]


def send_line(parts, axis):
    return [parts[0], *(send(parts[k], k, axis) for k in (2, 1, 3))]


def send_turned(parts):
    got = []
    for k in (2, 1, 3, 0):
        perm = [
            (z * GROUP + x, x * GROUP + (z + k) % GROUP) for z in range(GROUP) for x in range(GROUP)
        ]
        got.append(lax.ppermute(parts[k], ("fsdp_0", "rep"), perm))
    return got


def total(terms):
    return sum(g.astype(f32) for g in terms)


def add_pair(kept, other):
    return (kept.astype(f32) + other.astype(f32)).astype(bf16)


def norm_inverse(values):
    return lax.rsqrt(jnp.mean(values * values, axis=-1, keepdims=True) + EPS)


def norm_backward(values, inverse, gain, grads):
    scaled = grads * gain
    return inverse * scaled - values * (inverse * inverse * inverse) * jnp.mean(
        scaled * values, axis=-1, keepdims=True
    )


def make_tables():
    positions=jnp.arange(COUNT,dtype=f32)
    freqs=jnp.power(10000.0,-(jnp.arange(0,HEAD,2,dtype=f32)/HEAD))
    ang=positions[:,None]*freqs[None,:]
    c,s,o=jnp.cos(ang),jnp.sin(ang),jnp.zeros_like(ang)
    i=jnp.ones_like(ang)
    q=lambda a,b: [a,b,a,b]
    return jnp.stack([jnp.concatenate([c,c,c,c,c,c,i,i],1),jnp.concatenate([-s,o,-s,o,-s,o,o,o],1),jnp.concatenate([o,s,o,s,o,s,o,o],1)])


def near_copies(near, qkv, out, sems):
    copies = [pltpu.make_async_copy(near.at[:, pl.ds(0, QKV)], qkv, sems.at[GROUP])]
    for z in range(GROUP):
        copies.append(
            pltpu.make_async_copy(
                near.at[pl.ds(z * Q_COLS, Q_COLS), pl.ds(QKV, Q_COLS)],
                out.at[:, pl.ds(z * Q_COLS, Q_COLS)],
                sems.at[z],
            )
        )
    return copies

def turned(u, tables, at):
    low, high = tables[1, :, at : at + 128], tables[2, :, at : at + 128]
    return pltpu.roll(u, 96, 1) * low + pltpu.roll(u, 32, 1) * high

def paired(block):
    lane = lax.broadcasted_iota(jnp.int32, block.shape, 1)
    zero = jnp.zeros_like(block)
    return jnp.concatenate([jnp.where(lane < 64, block, zero), jnp.where(lane < 64, zero, block)], axis=0)

def doubled(kv):
    lane = lax.broadcasted_iota(jnp.int32, kv.shape, 1)
    swapped = pltpu.roll(kv, 64, 1)
    return jnp.where(lane < 64, kv, swapped), jnp.where(lane < 64, swapped, kv)

def softmax_parts(query, keys):
    scores = lax.dot_general(query, keys, NT, preferred_element_type=f32) * HEAD ** (-0.5)
    row = lax.broadcasted_iota(jnp.int32, scores.shape, 0) % COUNT
    col = lax.broadcasted_iota(jnp.int32, scores.shape, 1) % COUNT
    scores = jnp.where(row >= col, scores, masked)
    parts = []
    for i in range(2):
        part = scores[:, i * COUNT : (i + 1) * COUNT]
        expos = jnp.exp(part - jnp.max(part, axis=-1, keepdims=True))
        parts.append(expos / jnp.sum(expos, axis=-1, keepdims=True))
    return parts

def stacked(ref, rows):
    return jnp.concatenate([ref[rows, p * 128 : (p + 1) * 128] for p in range(4)], axis=0)

def attend_kernel(p0, p1, p2, p3, gain, tables, near, own, far1, far2, far3, first, joined, mixed, qkv, out, wide, sems):
    copies = near_copies(near, qkv, out, sems)
    for c in copies: c.start()
    for k, p in enumerate((p0, p1, p2, p3)):
        x = p[...].astype(f32)
        inverse = lax.rsqrt(jnp.mean(x * x, axis=-1, keepdims=True) + EPS)
        first[k * COUNT : (k + 1) * COUNT, :] = (x * inverse * gain[...]).astype(bf16)
    for c in copies: c.wait()
    wide[...] = jnp.dot(first[...], qkv[...], preferred_element_type=f32)

    @pl.loop(0, 4)
    def _(k):
        rows = pl.ds(pl.multiple_of(k * COUNT, COUNT), COUNT)
        for p in range(5):
            cols = slice(p * 128, (p + 1) * 128)
            at = 0 if p < 4 else 128
            u = wide[rows, cols]
            joined[rows, cols] = (u * tables[0, :, at : at + 128] + turned(u, tables, at)).astype(bf16)
        key, value = doubled(joined[rows, Q_COLS:].astype(f32))
        probs = softmax_parts(stacked(joined, rows), paired(key.astype(bf16)))
        probs = jnp.concatenate([p.astype(bf16) for p in probs], axis=1)
        got = jnp.dot(probs, paired(value.astype(bf16)), preferred_element_type=f32).astype(bf16)
        for p in range(4):
            mixed[rows, p * 128 : (p + 1) * 128] = got[p * COUNT : (p + 1) * COUNT]

    @pl.loop(0, WIDTH // 512)
    def _(n):
        cols = pl.ds(pl.multiple_of(n * 512, 512), 512)
        part = jnp.dot(mixed[...], out[:, cols], preferred_element_type=f32)
        own[:, cols] = part[:COUNT]
        for k, far in ((1, far1), (2, far2), (3, far3)):
            far[:, cols] = part[k * COUNT : (k + 1) * COUNT].astype(bf16)

def attend_group(pieces, gain, tables, near):
    any_=pl.BlockSpec(memory_space=pl.ANY); vm=pl.BlockSpec(memory_space=pltpu.VMEM)
    sd=jax.ShapeDtypeStruct; n=4*COUNT
    return pl.pallas_call(attend_kernel,in_specs=[vm]*4+[vm]*2+[any_],out_specs=[vm]*7,
        out_shape=[sd((COUNT,WIDTH),f32)]+[sd((COUNT,WIDTH),bf16)]*3+[sd((n,WIDTH),bf16),sd((n,QKV),bf16),sd((n,Q_COLS),bf16)],
        scratch_shapes=[pltpu.VMEM((WIDTH,QKV),bf16),pltpu.VMEM((Q_COLS,WIDTH),bf16),pltpu.VMEM((n,QKV),f32),pltpu.SemaphoreType.DMA((GROUP + 1,))],
        compiler_params=pltpu.CompilerParams(vmem_limit_bytes=VMEM_LIMIT),
        cost_estimate=pl.CostEstimate(flops=2*n*WIDTH*NEAR*2,bytes_accessed=2*(2*WIDTH*NEAR+3*n*WIDTH),transcendentals=n*HEADS*COUNT),
    )(*pieces,gain,tables,near)

def attend_back_kernel(place, d0, d1, d2, d3, p0, p1, p2, p3, second_gain, tables, near, first, joined, mixed,
                       own, far1, far2, far3, message_a, kept_a, message_b, kept_b, qkv, out, grads, mixed_grad, joined_grad, first_turned, mixed_turned, extra, sems):
    copies = near_copies(near, qkv, out, sems)
    for c in copies: c.start()
    z, y, core = place[0], place[1], place[2]
    for k, d in enumerate((d0, d1, d2, d3)):
        grads[k * COUNT : (k + 1) * COUNT, :] = d[...]
    inverses = []
    for p in (p0, p1, p2, p3):
        x = p[...].astype(f32)
        inverses.append(lax.rsqrt(jnp.mean(x * x, axis=-1, keepdims=True) + EPS))
    extra[...] = jnp.zeros_like(extra)
    for i in range(16):
        extra[16 + i : 17 + i, :] = second_gain[:, i * 128 : (i + 1) * 128]
    for c in copies: c.wait()
    mixed_grad[...] = lax.dot_general(grads[...], out[...], NT, preferred_element_type=f32).astype(bf16)

    @pl.loop(0, 4)
    def _(k):
        rows = pl.ds(pl.multiple_of(k * COUNT, COUNT), COUNT)
        key, value = doubled(joined[rows, Q_COLS:].astype(f32))
        keys, values = paired(key.astype(bf16)), paired(value.astype(bf16))
        query = stacked(joined, rows)
        upper = stacked(mixed_grad, rows)
        probs = softmax_parts(query, keys)
        prob_grad = lax.dot_general(upper, values, NT, preferred_element_type=f32)
        score_grad = []
        for i in range(2):
            part = prob_grad[:, i * COUNT : (i + 1) * COUNT]
            delta = jnp.sum(part * probs[i], axis=-1, keepdims=True)
            score_grad.append((probs[i] * (part - delta) * HEAD ** (-0.5)).astype(bf16))
        score_grad = jnp.concatenate(score_grad, axis=1)
        probs = jnp.concatenate([p.astype(bf16) for p in probs], axis=1)
        query_grad = jnp.dot(score_grad, keys, preferred_element_type=f32)
        key_grad = lax.dot_general(score_grad, query, TN, preferred_element_type=f32)
        value_grad = lax.dot_general(probs, upper, TN, preferred_element_type=f32)
        lane = lax.broadcasted_iota(jnp.int32, (COUNT, 128), 1)
        key_grad = key_grad[:COUNT] + pltpu.roll(key_grad[COUNT:], 64, 1)
        value_grad = pltpu.roll(value_grad[:COUNT], 64, 1) + value_grad[COUNT:]
        both = jnp.where(lane < 64, key_grad, value_grad)
        for p in range(5):
            at = 0 if p < 4 else 128
            w = query_grad[p * COUNT : (p + 1) * COUNT] if p < 4 else both
            joined_grad[rows, p * 128 : (p + 1) * 128] = (w * tables[0, :, at : at + 128] - turned(w, tables, at)).astype(bf16)

    @pl.loop(0, WIDTH // 512)
    def _(n):
        cols = pl.ds(pl.multiple_of(n * 512, 512), 512)
        part = lax.dot_general(joined_grad[...], qkv[cols, :], NT, preferred_element_type=f32)
        own[:, cols] = part[:COUNT]
        for k, far in ((1, far1), (2, far2), (3, far3)):
            far[:, cols] = part[k * COUNT : (k + 1) * COUNT].astype(bf16)
        total = jnp.zeros((1, 512), f32)
        for k, p in enumerate((p0, p1, p2, p3)):
            scaled = p[:, cols].astype(f32) * inverses[k]
            total = total + jnp.sum(part[k * COUNT : (k + 1) * COUNT] * scaled, axis=0, keepdims=True)
        for i in range(4):
            extra[pl.ds(n * 4 + i, 1), :] = total[:, i * 128 : (i + 1) * 128]

    for k in range(4):
        rows = slice(k * COUNT, (k + 1) * COUNT)
        first_turned[:, rows] = first[rows, :].T
        mixed_turned[:, rows] = mixed[rows, :].T

    @pl.loop(0, 4)
    def _(zi):
        dz = (zi + 4 - z) % 4
        rows = pl.ds(pl.multiple_of(zi * 512, 512), 512)
        left = jnp.dot(first_turned[rows, :], joined_grad[...], preferred_element_type=f32).astype(bf16)
        right = jnp.dot(mixed_turned[...], grads[:, rows], preferred_element_type=f32).astype(bf16)
        for yi in range(4):
            dy = (yi + 4 - y) % 4
            for owner in range(2):
                at = slice((yi * 2 + owner) * 64, (yi * 2 + owner + 1) * 64)
                def store(ref_a, ref_b):
                    ref_a[dz, dy, :, :QKV] = left[at]
                    ref_a[dz, dy, :, QKV:] = extra[...].astype(bf16)
                    ref_b[dy, dz] = right[at]
                @pl.when(core == owner)
                def _():
                    store(kept_a, kept_b)
                @pl.when(core != owner)
                def _():
                    store(message_a, message_b)

def attend_back_group(place, grads, pieces, second_gain, tables, near, first, joined, mixed):
    any_=pl.BlockSpec(memory_space=pl.ANY); vm=pl.BlockSpec(memory_space=pltpu.VMEM); sm=pl.BlockSpec(memory_space=pltpu.SMEM)
    sd=jax.ShapeDtypeStruct; n=4*COUNT
    return pl.pallas_call(attend_back_kernel,in_specs=[sm]+[vm]*10+[any_]+[vm]*3,out_specs=[vm]*8,
        out_shape=[sd((COUNT,WIDTH),f32)]+[sd((COUNT,WIDTH),bf16)]*3+[sd((4,4,64,QKV+128),bf16)]*2+[sd((4,4,64,Q_COLS),bf16)]*2,
        scratch_shapes=[pltpu.VMEM((WIDTH,QKV),bf16),pltpu.VMEM((Q_COLS,WIDTH),bf16),pltpu.VMEM((n,WIDTH),bf16),pltpu.VMEM((n,Q_COLS),bf16),pltpu.VMEM((n,QKV),bf16),
            pltpu.VMEM((WIDTH,n),bf16),pltpu.VMEM((Q_COLS,n),bf16),pltpu.VMEM((64,128),f32),pltpu.SemaphoreType.DMA((GROUP + 1,))],
        compiler_params=pltpu.CompilerParams(vmem_limit_bytes=VMEM_LIMIT),
        cost_estimate=pl.CostEstimate(flops=2*n*WIDTH*NEAR*3,bytes_accessed=2*(4*WIDTH*NEAR+6*n*WIDTH),transcendentals=n*HEADS*COUNT),
    )(place,*grads,*pieces,second_gain,tables,near,first,joined,mixed)

def ffn_kernel(order, p0, p1, p2, p3, d0, d1, d2, d3, weights, terms, hidden, wide_grad, rows, turned, gateup, down, wide, row_sem, grad_sem, gateup_sem, down_sem):
    count = p0.shape[0]
    blocks, depth = gateup.shape[0] // 64, 64
    lanes = 128
    row_copies = [pltpu.make_async_copy(p, rows.at[pl.ds(k * count, count)], row_sem.at[k]) for k, p in enumerate((p0, p1, p2, p3))]
    for c in row_copies: c.start()
    def gateup_copy(t):
        return pltpu.make_async_copy(
            weights.at[:, pl.ds(t * depth, depth), :],
            gateup.reshape(blocks, depth, 2 * FF_COLS).at[:, :, pl.ds(pl.multiple_of(t * lanes, lanes), lanes)],
            gateup_sem.at[t])
    tiles = 2 * FF_COLS // lanes
    for t in range(tiles): gateup_copy(t).start()
    grad_copies = [
        pltpu.make_async_copy(
            d, turned.at[pl.ds(k * count, count)], grad_sem.at[k]
        )
        for k, d in enumerate((d0, d1, d2, d3))
    ]
    for c in grad_copies:
        c.start()
    down_rows = FF_COLS // 8
    def down_copy(z, ct):
        return pltpu.make_async_copy(
            weights.at[pl.ds(z * 8, 8), pl.ds(tiles * depth + ct * down_rows, down_rows), :],
            down.reshape(8, down_rows, WIDTH).at[:, :, pl.ds((z * 4 + ct) * lanes, lanes)],
            down_sem.at[z * 4 + ct])
    for z in range(4):
        for ct in range(4): down_copy(z, ct).start()
    for c in row_copies: c.wait()

    @pl.loop(0, 2 * FF_COLS // 256)
    def _(t):
        gateup_copy(2 * t).wait()
        gateup_copy(2 * t + 1).wait()
        cols = pl.ds(pl.multiple_of(t * 256, 256), 256)
        wide[:, cols] = jnp.dot(rows[...], gateup[:, cols], preferred_element_type=f32)

    for c in grad_copies:
        c.wait()
    for z in range(4):
        for ct in range(4): down_copy(z, ct).wait()

    def back(start, width):
        cols = pl.ds(start, width)
        ups = pl.ds(pl.multiple_of(FF_COLS + start, 128), width)
        hidden_grad = lax.dot_general(turned[...], down[cols, :], NT, preferred_element_type=f32)
        gate = wide[:, cols]
        up_part = wide[:, ups]
        sigma = 1.0 / (1.0 + jnp.exp(-gate))
        act = gate * sigma
        hidden[:, cols] = (act * up_part).astype(bf16)
        wide_grad[:, cols] = (hidden_grad * up_part * sigma * (1.0 + gate * (1.0 - sigma))).astype(bf16)
        wide_grad[:, ups] = (hidden_grad * act).astype(bf16)

    @pl.loop(0, FF_COLS // 256)
    def _(t):
        back(pl.multiple_of(t * 256, 256), 256)
    if FF_COLS % 256:
        back(FF_COLS // 256 * 256, FF_COLS % 256)

    @pl.loop(0, WIDTH // 256)
    def _(n):
        cols = pl.ds(pl.multiple_of(n * 256, 256), 256)
        part = lax.dot_general(wide_grad[...], gateup[cols, :], NT, preferred_element_type=f32)
        part = part.astype(bf16)
        for k in range(GROUP):
            terms[(order[0] + k) % GROUP, :, cols] = part[k * count : (k + 1) * count]


def ffn(order, pieces, grads, weights):
    count=pieces[0].shape[0]; n=4*count
    any_=pl.BlockSpec(memory_space=pl.ANY); vm=pl.BlockSpec(memory_space=pltpu.VMEM)
    sd=jax.ShapeDtypeStruct
    tiles=2*FF_COLS//128
    return pl.pallas_call(
        ffn_kernel,
        in_specs=[pl.BlockSpec(memory_space=pltpu.SMEM)]+[any_]*9, out_specs=[vm]*3,
        out_shape=[sd((GROUP,count,WIDTH),bf16),sd((n,FF_COLS),bf16),sd((n,2*FF_COLS),bf16)],
        scratch_shapes=[pltpu.VMEM((n,WIDTH),bf16),pltpu.VMEM((n,WIDTH),bf16),pltpu.VMEM((WIDTH,2*FF_COLS),bf16),pltpu.VMEM((FF_COLS,WIDTH),bf16),pltpu.VMEM((n,2*FF_COLS),f32),
            pltpu.SemaphoreType.DMA((4,)),pltpu.SemaphoreType.DMA((4,)),pltpu.SemaphoreType.DMA((tiles,)),pltpu.SemaphoreType.DMA((16,))],
        compiler_params=pltpu.CompilerParams(vmem_limit_bytes=VMEM_LIMIT),
        cost_estimate=pl.CostEstimate(flops=2*n*WIDTH*FF_COLS*5,bytes_accessed=2*(3*WIDTH*FF_COLS+3*n*WIDTH+3*n*FF_COLS),transcendentals=n*FF_COLS),
    )(order.reshape(1),*pieces,*grads,weights)

def ffn_terms_kernel(place, *refs):
    own, refs = refs[:4], refs[4:]
    near, refs = refs[:4], refs[4:]
    grad_refs, refs = refs[:4], refs[4:]
    other_grads, hidden_refs, wide_refs, out = refs[0], refs[1:3], refs[3:5], refs[5]
    rows, turned, raw, grads, hidden, wide, tiles, blocks, in_sem, out_sem = refs[6:]
    core = place[2]
    span = 4 * COUNT
    depth = FF_COLS // 8
    steps = 2 * FF_COLS // 256
    row_loads = [
        pltpu.make_async_copy(p, raw.at[pl.ds(k * COUNT, COUNT)], in_sem.at[k])
        for k, p in enumerate((*own, *near))
    ]
    wide_loads = [
        pltpu.make_async_copy(w, wide.at[pl.ds(i * span, span)], in_sem.at[8 + i])
        for i, w in enumerate(wide_refs)
    ]
    late_loads = [
        pltpu.make_async_copy(w, hidden.at[pl.ds(i * span, span)], in_sem.at[10 + i])
        for i, w in enumerate(hidden_refs)
    ]
    late_loads += [
        pltpu.make_async_copy(
            d, grads.at[pl.ds(k * COUNT, COUNT)], in_sem.at[12 + k]
        )
        for k, d in enumerate(grad_refs)
    ]
    late_loads.append(pltpu.make_async_copy(other_grads, grads.at[pl.ds(span, span)], in_sem.at[16]))
    for c in (*row_loads, *wide_loads, *late_loads):
        c.start()
    for k, c in enumerate(row_loads):
        c.wait()
        cols = slice(k * COUNT, (k + 1) * COUNT)
        both = raw[cols, :].T.reshape(16, 2, 64, COUNT)
        rows[:, cols] = jnp.where(core == 0, both[:, 0], both[:, 1]).reshape(WIDTH // 2, COUNT)
    for c in wide_loads:
        c.wait()

    def tile_store(t):
        return pltpu.make_async_copy(
            tiles.at[t % 2],
            out.at[:, pl.ds(pl.multiple_of(t * 128, 128), 128), :],
            out_sem.at[t % 2],
        )

    @pl.loop(0, steps)
    def _(t):
        @pl.when(t >= 2)
        def _():
            tile_store(t - 2).wait()

        cols = pl.ds(pl.multiple_of(t * 256, 256), 256)
        part = jnp.dot(rows[...], wide[:, cols], preferred_element_type=f32).astype(bf16)
        part = part.reshape(16, 64, 256)
        for i in range(2):
            tiles[t % 2, :, i * 64 : (i + 1) * 64, :] = part[:, :, i * 128 : (i + 1) * 128]
        tile_store(t).start()

    for c in late_loads:
        c.wait()
    for k in range(8):
        cols = slice(k * COUNT, (k + 1) * COUNT)
        both = hidden[cols, :].T.reshape(GROUP, 2, depth, COUNT)
        turned[:, cols] = jnp.where(core == 0, both[:, 0], both[:, 1]).reshape(FF_COLS // 2, COUNT)

    def block_store(t):
        return pltpu.make_async_copy(
            blocks.at[t % 2],
            out.at[
                pl.ds(t // 2 * GROUP, GROUP),
                pl.ds(pl.multiple_of(FF_COLS + t % 2 * 2 * depth, 32), 2 * depth),
                :,
            ],
            out_sem.at[2 + t % 2],
        )

    @pl.loop(0, 8)
    def _(t):
        @pl.when(t >= 2)
        def _():
            block_store(t - 2).wait()

        cols = pl.ds(pl.multiple_of(t * 256, 256), 256)
        part = jnp.dot(turned[...], grads[:, cols], preferred_element_type=f32).astype(bf16)
        part = part.reshape(GROUP, depth, 256)
        for i in range(2):
            blocks[t % 2, :, i * depth : (i + 1) * depth, :] = part[:, :, i * 128 : (i + 1) * 128]
        block_store(t).start()

    tile_store(steps - 2).wait()
    tile_store(steps - 1).wait()
    block_store(6).wait()
    block_store(7).wait()


def ffn_terms(place, pieces, other_pieces, grads, other_grads, hidden, other_hidden, wide, other_wide):
    n = 8 * COUNT
    any_ = pl.BlockSpec(memory_space=pl.ANY)
    return pl.pallas_call(
        ffn_terms_kernel,
        in_specs=[pl.BlockSpec(memory_space=pltpu.SMEM)] + [any_] * 17,
        out_specs=any_,
        out_shape=jax.ShapeDtypeStruct((16, 2112, 128), bf16),
        scratch_shapes=[
            pltpu.VMEM((WIDTH // 2, n), bf16),
            pltpu.VMEM((FF_COLS // 2, n), bf16),
            pltpu.VMEM((n, WIDTH), bf16),
            pltpu.VMEM((n, WIDTH), bf16),
            pltpu.VMEM((n, FF_COLS), bf16),
            pltpu.VMEM((n, 2 * FF_COLS), bf16),
            pltpu.VMEM((2, 16, 128, 128), bf16),
            pltpu.VMEM((2, GROUP, FF_COLS // 4, 128), bf16),
            pltpu.SemaphoreType.DMA((17,)),
            pltpu.SemaphoreType.DMA((4,)),
        ],
        compiler_params=pltpu.CompilerParams(vmem_limit_bytes=VMEM_LIMIT),
        cost_estimate=pl.CostEstimate(
            flops=3 * n * WIDTH * FF_COLS,
            bytes_accessed=3 * WIDTH * FF_COLS + 4 * n * WIDTH + 6 * n * FF_COLS,
            transcendentals=0,
        ),
    )(place, *pieces, *other_pieces, *grads, other_grads, hidden, other_hidden, wide, other_wide)


def ffn_out_kernel(hidden, weights, own, far1, far2, far3, down, down_sem):
    count=own.shape[0]
    depth = 64
    tiles = 2 * FF_COLS // 128
    down_rows = FF_COLS // 8
    def down_copy(z, ct):
        return pltpu.make_async_copy(
            weights.at[pl.ds(z * 8, 8), pl.ds(tiles * depth + ct * down_rows, down_rows), :],
            down.reshape(8, down_rows, WIDTH).at[:, :, pl.ds((z * 4 + ct) * 128, 128)],
            down_sem.at[z * 4 + ct])
    for z in range(4):
        for ct in range(4): down_copy(z, ct).start()
    for z in range(4):
        for ct in range(4): down_copy(z, ct).wait()
        cols = slice(z * 512, (z + 1) * 512)
        part = jnp.dot(hidden[...], down[:, cols], preferred_element_type=f32)
        own[:, cols] = part[:count]
        for k, far in ((1, far1), (2, far2), (3, far3)):
            far[:, cols] = part[k * count : (k + 1) * count].astype(bf16)
def ffn_out(hidden, weights):
    n=hidden.shape[0]; count=n//4
    any_=pl.BlockSpec(memory_space=pl.ANY); vm=pl.BlockSpec(memory_space=pltpu.VMEM)
    sd=jax.ShapeDtypeStruct
    return pl.pallas_call(ffn_out_kernel,in_specs=[vm,any_],out_specs=[vm]*4,
        out_shape=[sd((count,WIDTH),f32)]+[sd((count,WIDTH),bf16)]*3,
        scratch_shapes=[pltpu.VMEM((FF_COLS,WIDTH),bf16),pltpu.SemaphoreType.DMA((16,))],
        compiler_params=pltpu.CompilerParams(vmem_limit_bytes=VMEM_LIMIT),
        cost_estimate=pl.CostEstimate(flops=2*n*WIDTH*FF_COLS,bytes_accessed=2*(WIDTH*FF_COLS+n*WIDTH+n*FF_COLS),transcendentals=0),
    )(hidden,weights)
def adamw(weight, grad, moment, second, rate, decay):
    moment = beta_one * moment + (1.0 - beta_one) * grad
    second = beta_two * second + (1.0 - beta_two) * grad * grad
    scale_one = 1.0 / (1.0 - beta_one**STEP)
    scale_two = 1.0 / (1.0 - beta_two**STEP)
    weight = weight - rate * (
        moment * scale_one / (jnp.sqrt(second * scale_two) + adam_epsilon) + decay * weight
    )
    return (moment, second, weight)


def chosen(order, pieces):
    low = jnp.where(order == 0, pieces[0], pieces[1])
    high = jnp.where(order == 2, pieces[2], pieces[3])
    return jnp.where(order < 2, low, high)


def adam_gathered_kernel(piece, weight, moment, second, m_out, s_out, w_out):
    columns = weight.shape[1]
    tiles = columns // (2 * GROUP * 128)
    for part in range(2):
        for j in range(GROUP):
            for t in range(tiles):
                at = (part * GROUP + j) * tiles + t
                cols = slice(at * 128, (at + 1) * 128)
                m_out[:, cols], s_out[:, cols], w_out[:, cols] = adamw(
                    weight[:, cols],
                    piece[j, part * tiles + t].astype(f32),
                    moment[:, cols],
                    second[:, cols],
                    matrix_rate,
                    matrix_decay,
                )


def adam_gathered(gathered, weight, moment, second):
    rows, columns = weight.shape
    tile = rows // 2
    wide = pl.BlockSpec((tile, columns), lambda i: (i, 0))
    piece = pl.BlockSpec((GROUP, columns // (GROUP * 128), tile, 128), lambda i: (0, 0, i, 0))
    return pl.pallas_call(
        adam_gathered_kernel,
        grid=(2,),
        in_specs=[piece] + [wide] * 3,
        out_specs=[wide] * 3,
        out_shape=[jax.ShapeDtypeStruct(weight.shape, f32)] * 3,
        compiler_params=pltpu.CompilerParams(vmem_limit_bytes=VMEM_LIMIT),
        cost_estimate=pl.CostEstimate(
            flops=12 * rows * columns, bytes_accessed=26 * rows * columns, transcendentals=0
        ),
    )(gathered.reshape(GROUP, -1, rows, 128), weight, moment, second)


def adam_near_kernel(order, p0, p1, p2, p3, *refs):
    i = pl.program_id(0)
    qkv, out, down = refs[0:3], refs[3:6], refs[6:9]
    qkv_new, out_new, down_new = refs[9:12], refs[12:15], refs[15:18]
    rows, down_rows = qkv[0].shape[0], down[0].shape[0]
    last = Q_COLS // 128
    down_at = (last + 2) * 2 * rows
    out_at = down_at + last * down_rows

    def grad(j, at, size):
        at = pl.ds(pl.multiple_of(at, 16), size)
        which = (j + GROUP - order[0]) % GROUP
        return chosen(which, [p[at, :].astype(f32) for p in (p0, p1, p2, p3)])

    def step(old, new, start, terms):
        cols = slice(start, start + terms.shape[1])
        new[0][:, cols], new[1][:, cols], new[2][:, cols] = adamw(
            old[0][:, cols], terms, old[1][:, cols], old[2][:, cols], matrix_rate, matrix_decay
        )

    both = []
    for j in range(GROUP):
        for t in range(last):
            at = (2 * t + i) * rows
            step(qkv, qkv_new, j * Q_COLS + t * 128, grad(j, at, rows))
            step(out, out_new, j * Q_COLS + t * 128, grad(j, out_at + at, rows))
        both.append(grad(j, (2 * last + i) * rows, rows))
    step(qkv, qkv_new, WIDTH, jnp.concatenate([b[:, :KV_COLS] for b in both], axis=1))
    step(qkv, qkv_new, WIDTH + KV_WIDTH, jnp.concatenate([b[:, KV_COLS:] for b in both], axis=1))
    for j in range(2):
        for t in range(last):
            terms = grad(2 * i + j, down_at + t * down_rows, down_rows)
            step(down, down_new, j * Q_COLS + t * 128, terms)


def adam_near(order, pieces, *states):
    size = sum(a.size for a in states)
    whole = pl.BlockSpec(pieces[0].shape, lambda i, order: (0, 0), pipeline_mode=pl.Buffered(1))
    blocks = [
        pl.BlockSpec((a.shape[0] // 2, a.shape[1]), lambda i, order: (i, 0)) for a in states[:6]
    ]
    blocks += [
        pl.BlockSpec((a.shape[0], a.shape[1] // 2), lambda i, order: (0, i)) for a in states[6:]
    ]
    return pl.pallas_call(
        adam_near_kernel,
        grid_spec=pltpu.PrefetchScalarGridSpec(
            num_scalar_prefetch=1,
            grid=(2,),
            in_specs=[whole] * 4 + blocks,
            out_specs=blocks,
        ),
        out_shape=[jax.ShapeDtypeStruct(a.shape, f32) for a in states],
        compiler_params=pltpu.CompilerParams(vmem_limit_bytes=VMEM_LIMIT),
        cost_estimate=pl.CostEstimate(flops=4 * size, bytes_accessed=9 * size, transcendentals=0),
    )(order.reshape(1), *pieces, *states)


def in_tiles(block):
    rows, columns = block.shape
    return block.reshape(rows, columns // 128, 128).transpose(1, 0, 2).reshape(-1, 128)


def body(
    tokens,
    cotangent,
    lengths,
    qkv_weight,
    qkv_moment,
    qkv_second,
    out_weight,
    out_moment,
    out_second,
    gateup_weight,
    gateup_moment,
    gateup_second,
    down_weight,
    down_moment,
    down_second,
    gains,
    gain_moment,
    gain_second,
):
    order = lax.axis_index("rep")
    spot = jnp.stack([lax.axis_index(a) for a in FSDP_REP]).astype(jnp.int32)
    inputs = tokens.astype(f32)
    positions = jnp.arange(COUNT, dtype=jnp.int32)
    valid = (positions < lengths[0]).astype(f32)[:, None]
    result_grad = cotangent.astype(f32) * valid
    output_low = result_grad.astype(bf16)
    tables = make_tables()

    def cut(weight, start, width):
        return lax.dynamic_slice_in_dim(weight, start + order * width, width, axis=1).astype(bf16)

    quarter = WIDTH // GROUP
    down_rows = down_weight.shape[0]
    near_block = jnp.concatenate(
        [
            cut(qkv_weight, 0, Q_COLS),
            cut(qkv_weight, WIDTH, KV_COLS),
            cut(qkv_weight, WIDTH + KV_WIDTH, KV_COLS),
            turn(cut(out_weight, 0, quarter)),
        ],
        axis=1,
    )
    near = lax.all_gather(near_block, FSDP, axis=0, tiled=True)
    pieces = gather_rows(tokens)
    pieces, output_low = lax.optimization_barrier((pieces, output_low))
    group_grads = gather_rows(output_low)
    far_block = jnp.concatenate(
        [
            in_tiles(cut(gateup_weight, 0, FF_COLS)),
            in_tiles(cut(gateup_weight, FF, FF_COLS)),
            in_tiles(turn(cut(down_weight, 0, quarter))),
        ]
    )
    near, far_block, pieces, group_grads = lax.optimization_barrier(
        (near, far_block, pieces, group_grads)
    )
    far = lax.all_gather(far_block, FSDP, axis=0)

    *branch, first, joined, mixed = attend_group(pieces, gains[:1], tables, near)
    middle = inputs + scatter_rows(*branch)
    second_inverse = norm_inverse(middle)
    second = gather_rows((middle * second_inverse * gains[1]).astype(bf16))
    other_grads = swap(jnp.concatenate(group_grads))
    other_second = [swap(p) for p in second]
    second, other_second, other_grads = lax.optimization_barrier(
        (second, other_second, other_grads)
    )
    second_terms, hidden, wide_grad = ffn(order, second, group_grads, far)
    second_grad = lax.psum_scatter(
        second_terms.reshape(-1, WIDTH), "rep", scatter_dimension=0, tiled=True
    ).astype(f32)
    other_hidden, other_wide = swap(hidden), swap(wide_grad)
    far_terms = ffn_terms(
        spot, second, other_second, group_grads, other_grads, hidden, other_hidden, wide_grad, other_wide
    )
    far_piece = lax.psum_scatter(
        far_terms.reshape(-1, 128), FSDP[:2], scatter_dimension=0, tiled=True
    )
    second_gain_grad = jnp.sum(second_grad * middle * second_inverse, axis=0, keepdims=True)
    middle_grad = result_grad + norm_backward(middle, second_inverse, gains[1], second_grad)
    branch_low, hidden = lax.optimization_barrier((middle_grad.astype(bf16), hidden))
    branch_grads = gather_rows(branch_low)
    output_terms = ffn_out(hidden, far)
    branch_grads, output_terms = lax.optimization_barrier((branch_grads, output_terms))
    output = scatter_rows(*output_terms)

    *first_terms, message_a, kept_a, message_b, kept_b = attend_back_group(
        spot, branch_grads, pieces, second_gain_grad, tables, near, first, joined, mixed
    )
    message_a, message_b, output = lax.optimization_barrier((message_a, message_b, output))
    block_output = ((middle + output) * valid).astype(bf16)
    other_a, other_b = swap(message_a), swap(message_b)
    first_terms = hand_out(*first_terms)
    terms_a = send_line(add_pair(kept_a, other_a), "fsdp_0")
    terms_b = send_line(add_pair(kept_b, other_b), "fsdp_1")
    first_terms, terms_a, terms_b, far_piece = lax.optimization_barrier(
        (first_terms, terms_a, terms_b, far_piece)
    )
    depth = gateup_weight.shape[0]
    wide_rows = 2 * FF_COLS // 128 * depth
    wide_pieces = lax.all_gather(far_piece[:wide_rows], "rep")
    down_away = turn(far_piece[wide_rows:])
    terms_b = send_turned(total(terms_b).astype(bf16))
    terms_a = send_line(total(terms_a).astype(bf16), "fsdp_1")
    tiles_a = in_tiles(total(terms_a).astype(bf16))
    tiles_b = in_tiles(total(terms_b).astype(bf16))
    parts, wide_pieces = lax.optimization_barrier(((tiles_a, down_away, tiles_b), wide_pieces))
    near_pieces = share(jnp.concatenate(parts))
    gateup_new = adam_gathered(wide_pieces, gateup_weight, gateup_moment, gateup_second)
    near_new = adam_near(
        order,
        near_pieces,
        qkv_weight,
        qkv_moment,
        qkv_second,
        out_weight,
        out_moment,
        out_second,
        down_weight,
        down_moment,
        down_second,
    )
    qkv_new, out_new, down_new = near_new[0:3], near_new[3:6], near_new[6:9]
    gain_at = QKV // 128 * depth
    gain_grad = sum(p[gain_at : gain_at + 2 * WIDTH // 128].astype(f32) for p in near_pieces)
    first_grad = total(first_terms)
    input_grad = middle_grad + norm_backward(inputs, norm_inverse(inputs), gains[0], first_grad)
    gain_new = adamw(gains, gain_grad.reshape(gains.shape), gain_moment, gain_second, gain_rate, 0.0)
    return (
        block_output,
        input_grad,
        *qkv_new,
        *out_new,
        *gateup_new,
        *down_new,
        *gain_new,
    )


def solution(mesh):
    finer = Mesh(
        mesh.devices.reshape(4, 4, 2, mesh.shape["rep"]), ("fsdp_0", "fsdp_1", "fsdp_2", "rep")
    )
    row = P(FSDP_REP, None)
    weight = P(FSDP, None)
    return jax.shard_map(
        body,
        mesh=finer,
        in_specs=(row, row, P(FSDP_REP)) + (weight,) * 12 + (P(),) * 3,
        out_specs=(row, row) + (weight,) * 12 + (P(),) * 3,
        check_vma=False,
    )
```
